768 devices in a mesh: dp: 64 (over x, y, core), group: 12 (over z).
Axes of the slice: x: 4, y: 8, z: 12, core: 2. Of those that a mesh axis runs over, the one named last changes fastest.
Arguments:
- grad: float32 [12, 9216, 128], P('group', 'dp'), may hold values from -6000 to 6000
- momentum: float32 [12, 9216, 128], P('group', 'dp'), may hold values from -6 to 6
Outputs:
- momentum_out: float32 [12, 9216, 128], P('group', 'dp')
- update: bfloat16 [12, 9216, 128], P('group', 'dp')
The draws below stay inside these ranges and needn't reach their ends.
All inputs are finite; a program needn't handle non-finite values.
Results may differ from the reference program's by a relative error of at most 0.002.
The reference program's roundings to bfloat16 on the way count: a program that leaves them out, or rounds other values in their place, can miss the bound.
Values may be sent and summed in bfloat16 or wider, within the bound.
No kernel may reach another device: no remote copies, remote signals or barrier semaphores. Data moves between devices by JAX's collectives and lax.ppermute only.
A program may use at most 32 MiB of HBM per device.

```python
import math
import jax
import jax.numpy as jnp
from jax import lax

D = 2048
ROWS = 576
ITERS = 2
LAYERS = 12


def draw_grad(key, part):
    key = jax.random.fold_in(key, 11)
    key_rows, key_cols, key_values = jax.random.split(key, 3)
    row_scale = jnp.exp(jax.random.uniform(key_rows, (LAYERS, D, 1)) * jnp.log(10.0))
    col_scale = jnp.exp(jax.random.uniform(key_cols, (LAYERS, 1, ROWS)) * jnp.log(10.0))
    position = jnp.arange(D, dtype=jnp.float32) / (D - 1)
    layer_pos = jnp.arange(LAYERS, dtype=jnp.float32) / max(LAYERS - 1, 1)
    rising = jnp.exp(jnp.log(3.0) * (position[None, :, None] + layer_pos[:, None, None]))
    values = jnp.clip(jax.random.normal(key_values, (LAYERS, D, ROWS)), -5.0, 5.0)
    matrix = (values * row_scale * col_scale * rising).astype(jnp.float32)
    return matrix.reshape(LAYERS, D * ROWS // 128, 128)


def block_scale(stream_key, dims, cuts, least, top_value):
    level = 1.0
    for dim, parts in cuts:
        draws = jax.random.uniform(jax.random.fold_in(jax.random.fold_in(stream_key, 6), dim), (parts,), jnp.float32, least / len(cuts), top_value / len(cuts))
        level = level * jnp.repeat(jnp.exp(draws), dims[dim] // parts).reshape((-1,) + (1,) * (len(dims) - 1 - dim))
    return level


def scatter_about(own_key, extent, deviation, most, pieces=(), held_as=jnp.bfloat16):
    values = deviation * jax.random.normal(own_key, extent, jnp.float32)
    if pieces:
        values = values * block_scale(own_key, extent, pieces, -0.22, 0.18)
    return jnp.clip(values, -most, most).astype(held_as)


def setup_inputs(seed: int = 0) -> dict:
    streams_of = jax.random.split(jax.random.key(seed), 3)
    grad = draw_grad(jax.random.fold_in(streams_of[2], 71), 0)
    momentum = scatter_about(streams_of[1], (LAYERS, D * ROWS // 128, 128), 1.0, 6.0, ((0, 12), (1, 64)), jnp.float32)
    return dict(grad=grad, momentum=momentum)


momentum_rate = 0.95
target_rms = 0.5
coef_first = 3.4445
coef_second = -4.775
coef_third = 2.0315

def reference(grad, momentum):
    entries = LAYERS * ROWS * D
    square = jnp.sum(grad * grad)
    grad_scale = target_rms / (jnp.sqrt(square / entries) + 1e-06)
    momentum_out = momentum_rate * momentum + grad_scale * grad
    nudged = grad_scale * grad + momentum_rate * momentum_out
    update_scale = 0.2 * math.sqrt(max(ROWS, D))

    def per_layer(nudged_layer):
        unorm = jnp.sqrt(jnp.sum(nudged_layer * nudged_layer))
        iterate = (nudged_layer / (unorm + 1e-07)).astype(jnp.bfloat16).reshape(D, ROWS)
        result = None
        for step in range(ITERS):
            gram_matrix = jnp.dot(iterate.T, iterate, preferred_element_type=jnp.float32)
            gram_low = gram_matrix.astype(jnp.bfloat16)
            polynomial = (coef_second * gram_matrix + coef_third * jnp.dot(gram_low, gram_low, preferred_element_type=jnp.float32)).astype(jnp.bfloat16)
            combined = coef_first * iterate.astype(jnp.float32) + jnp.dot(iterate, polynomial, preferred_element_type=jnp.float32)
            if step + 1 < ITERS:
                iterate = combined.astype(jnp.bfloat16)
            else:
                result = (update_scale * combined).astype(jnp.bfloat16)
        return result.reshape(D * ROWS // 128, 128)
    update = lax.map(per_layer, nudged)
    return (momentum_out, update)
```

```python
import functools
import math

import jax
import jax.numpy as jnp
import numpy as np
from jax import lax
from jax.experimental import pallas as pl
from jax.experimental.pallas import tpu as pltpu
from jax.sharding import Mesh, PartitionSpec as P

ROWS = 576
ITERS = 2

momentum_rate = 0.95
target_rms = 0.5
coef_first = 3.4445
coef_second = -4.775
coef_third = 2.0315

f32, bf16 = jnp.float32, jnp.bfloat16
VMEM = pl.BlockSpec(memory_space=pltpu.VMEM)
SMEM = pl.BlockSpec(memory_space=pltpu.SMEM)
NT = (((1,), (1,)), ((), ()))


def two_sum(a, b):
    s = a + b
    t = s - a
    return s, (a - (s - t)) + (b - t)


def fast_two_sum(a, b):
    s = a + b
    return s, b - (s - a)


def split(a):
    t = 4097.0 * a
    high = t - (t - a)
    return high, a - high


def two_prod(a, b):
    p = a * b
    ah, al = split(a)
    bh, bl = split(b)
    return p, ((ah * bh - p) + ah * bl + al * bh) + al * bl


def dd_add(a, b):
    s, e = two_sum(a[0], b[0])
    return fast_two_sum(s, e + (a[1] + b[1]))


def dd_mul(a, b):
    p, e = two_prod(a[0], b[0])
    return fast_two_sum(p, e + (a[0] * b[1] + a[1] * b[0]))


def dd_const(value):
    high = np.float32(value)
    return float(high), float(np.float32(value - float(high)))


def tile_tree(values):
    while len(values) > 1:
        paired = [dd_add(values[i], values[i + 1]) for i in range(0, len(values) - 1, 2)]
        values = paired + ([values[-1]] if len(values) % 2 else [])
    return values[0]


def all_lanes(a):
    for axis, shifts in ((0, (4, 2, 1)), (1, (64, 32, 16, 8, 4, 2, 1))):
        for shift in shifts:
            a = dd_add(a, (pltpu.roll(a[0], shift, axis), pltpu.roll(a[1], shift, axis)))
    return a


def pack_rows(values):
    row = lax.broadcasted_iota(jnp.int32, (8, 128), 0)
    tile = jnp.zeros((8, 128), f32)
    for i, (high, low) in enumerate(values):
        tile = jnp.where(row == i, high, jnp.where(row == i + 4, low, tile))
    return tile


def unpack(tile):
    return tile, pltpu.roll(tile, 4, 0)


def repack(pair):
    row = lax.broadcasted_iota(jnp.int32, (8, 128), 0)
    return jnp.where(row < 4, pair[0], pltpu.roll(pair[1], 4, 0))


def sums_kernel(copies, grad_ref, momentum_ref, out_ref):
    rows = grad_ref.shape[1]
    gg, gm, mm = [], [], []
    for i in range(0, rows, 8):
        g = grad_ref[0, i : i + 8, :]
        m = momentum_ref[0, i : i + 8, :]
        gg.append(two_prod(g, g))
        gm.append(two_prod(g, m))
        mm.append(two_prod(m, m))
    tile = pack_rows([all_lanes(tile_tree(v)) for v in (gg, gm, mm)])
    for i in range(copies):
        out_ref[i] = tile


def combine_kernel(copies, in_ref, out_ref):
    tile = repack(tile_tree([unpack(in_ref[i]) for i in range(in_ref.shape[0])]))
    for i in range(copies):
        out_ref[i] = tile


def scale_kernel(entries, groups, copies, group_ref, in_ref, grad_ref, momentum_ref, momentum_out_ref, out_ref):
    group = group_ref[0]
    whole = tile_tree([unpack(in_ref[i]) for i in range(in_ref.shape[0])])
    own = tile_tree([unpack(in_ref[group + i]) for i in range(0, in_ref.shape[0], groups)])
    square = whole[0][0:1]
    grad_scale = target_rms / (jnp.sqrt(square / entries) + 1e-06)
    rate = float(np.float32(momentum_rate))
    gg = (own[0][0:1], own[1][0:1])
    gm = (own[0][1:2], own[1][1:2])
    mm = (own[0][2:3], own[1][2:3])
    factor_high, factor_low = dd_const(1.0 + rate)
    ones = jnp.ones_like(grad_scale)
    a = two_prod(grad_scale, factor_high * ones)
    a = fast_two_sum(a[0], a[1] + grad_scale * factor_low)
    b = tuple(v * ones for v in dd_const(rate * rate))
    ag = dd_mul(a, gg)
    cross = dd_mul(dd_mul((2.0 * a[0], 2.0 * a[1]), b), gm)
    total = dd_add(dd_add(dd_mul(a, ag), dd_mul(dd_mul(b, b), mm)), cross)
    unorm = jnp.sqrt(jnp.maximum(total[0], 0.0))
    scaled_grad = grad_scale * grad_ref[0]
    momentum_out = momentum_rate * momentum_ref[0] + scaled_grad
    nudged = scaled_grad + momentum_rate * momentum_out
    momentum_out_ref[0] = momentum_out
    iterate = (nudged / (unorm + 1e-07)).astype(bf16)
    for i in range(copies):
        out_ref[i] = iterate


def transpose_kernel(copies, in_ref, out_ref, flat_ref):
    blocks, rows = in_ref.shape[:2]
    for i in range(blocks):
        flat_ref[i * rows : (i + 1) * rows, :] = in_ref[i].astype(f32)
    half = blocks * rows // 9
    for j in range(9):
        turned = flat_ref[pl.ds(j, half, stride=9), :].T.astype(bf16)
        for i in range(copies):
            if j < 4:
                out_ref[i, 128 * j : 128 * j + 128, 0:half] = turned
            elif j == 4:
                out_ref[i, 512:576, 0:half] = turned[0:64]
                out_ref[i, 0:64, half : 2 * half] = turned[64:128]
            else:
                out_ref[i, 128 * j - 576 : 128 * j - 448, half : 2 * half] = turned


def own_load(flat_ref, pairs):
    low = lax.broadcasted_iota(jnp.int32, (pairs, 128), 1) < 64
    flat = [flat_ref[pl.ds(j, pairs, stride=9), :] for j in range(9)]
    turned = [pltpu.roll(flat[j], 64, 1) for j in range(4, 9)]
    even = flat[:4] + [flat[4]]
    odd = [jnp.where(low, turned[k], turned[k + 1]) for k in range(4)] + [turned[4]]
    return jnp.concatenate([jnp.concatenate(even, 1), jnp.concatenate(odd, 1)], 0)[:, :ROWS]


def own_store(flat_ref, value, pairs):
    value = jnp.concatenate([value, jnp.zeros((2 * pairs, 64), f32)], 1)
    low = lax.broadcasted_iota(jnp.int32, (pairs, 128), 1) < 64
    even = [value[:pairs, 128 * j : 128 * j + 128] for j in range(5)]
    odd = [pltpu.roll(value[pairs:, 128 * j : 128 * j + 128], 64, 1) for j in range(5)]
    flat = even[:4] + [jnp.where(low, even[4], odd[0])]
    flat += [jnp.where(low, odd[k], odd[k + 1]) for k in range(4)]
    for j in range(9):
        flat_ref[pl.ds(j, pairs, stride=9), :] = flat[j]


def iterate_kernel(update_scale, mine_ref, other_ref, own_ref, out_ref, poly_ref, next_ref, flat_ref):
    blocks = [(r, i) for r in (mine_ref, other_ref) for i in range(r.shape[0])]
    pairs = own_ref.shape[0] // 9

    def gram(get):
        total = None
        for i in range(len(blocks)):
            v = get(i)
            d = lax.dot_general(v, v, NT, preferred_element_type=f32)
            total = d if total is None else total + d
        return total

    def poly(gram_matrix):
        low = gram_matrix.astype(bf16)
        squared = jnp.dot(low, low, preferred_element_type=f32)
        return (coef_second * gram_matrix + coef_third * squared).astype(bf16)

    poly_ref[...] = poly(gram(lambda i: blocks[i][0][blocks[i][1]]))
    for i, (r, k) in enumerate(blocks):
        v = r[k]
        product = jnp.dot(poly_ref[...], v, preferred_element_type=f32)
        next_ref[i] = (coef_first * v.astype(f32) + product).astype(bf16)
    flat_ref[...] = own_ref[...].astype(f32)
    own = own_load(flat_ref, pairs)
    product = jnp.dot(own.astype(bf16), poly_ref[...], preferred_element_type=f32)
    own = (coef_first * own + product).astype(bf16)
    poly_ref[...] = poly(gram(lambda i: next_ref[i]))
    product = jnp.dot(own, poly_ref[...], preferred_element_type=f32)
    own_store(flat_ref, update_scale * (coef_first * own.astype(f32) + product), pairs)
    out_ref[0] = flat_ref[...].astype(bf16)


def kernel(body, name, out, n_in, scratch=(), in_specs=None):
    return pl.pallas_call(
        body,
        name=name,
        out_shape=out,
        in_specs=in_specs or [VMEM] * n_in,
        out_specs=jax.tree.map(lambda _: VMEM, out),
        scratch_shapes=list(scratch),
        compiler_params=pltpu.CompilerParams(vmem_limit_bytes=48 * 2**20),
    )


def local(entries, update_scale, sizes, grad, momentum):
    nx, ny, nc, ng = sizes
    rows = grad.shape[1]
    shape = jax.ShapeDtypeStruct
    sums = kernel(functools.partial(sums_kernel, nx * ny), "sums", shape((nx * ny, 8, 128), f32), 2)(grad, momentum)
    sums = lax.all_to_all(sums, ("x", "y"), 0, 0)
    sums = kernel(functools.partial(combine_kernel, nc * ng), "combine", shape((nc * ng, 8, 128), f32), 1)(sums)
    sums = lax.all_to_all(sums, ("core", "group"), 0, 0)
    group = lax.axis_index("group").astype(jnp.int32).reshape(1)
    momentum_out, iterate = kernel(
        functools.partial(scale_kernel, entries, ng, ny),
        "scale",
        (shape(grad.shape, f32), shape((ny, rows, 128), bf16)),
        4,
        in_specs=[SMEM, VMEM, VMEM, VMEM],
    )(group, sums, grad, momentum)
    own = iterate[0]
    gathered = lax.all_to_all(iterate, "y", 0, 0)
    columns = ny * rows * 128 // ROWS
    turned = kernel(
        functools.partial(transpose_kernel, nx),
        "turn",
        shape((nx, ROWS, columns), bf16),
        1,
        scratch=[pltpu.VMEM((ny * rows, 128), f32)],
    )(gathered)
    mine = lax.all_to_all(turned, "x", 0, 0)
    other = lax.ppermute(mine, "core", [(0, 1), (1, 0)])
    update = kernel(
        functools.partial(iterate_kernel, update_scale),
        "newton",
        shape(grad.shape, bf16),
        3,
        scratch=[
            pltpu.VMEM((ROWS, ROWS), bf16),
            pltpu.VMEM((2 * nx, ROWS, columns), bf16),
            pltpu.VMEM((rows, 128), f32),
        ],
    )(mine, other, own)
    return momentum_out, update


def solution(mesh):
    sizes = (4, 8, 2, 12)
    split_mesh = Mesh(mesh.devices.reshape(sizes), ("x", "y", "core", "group"))
    spec = P("group", ("x", "y", "core"), None)

    def run(grad, momentum):
        entries = grad.size
        layers, flat_rows, _ = grad.shape
        width = flat_rows * 128 // ROWS
        update_scale = 0.2 * math.sqrt(max(ROWS, width))
        return jax.shard_map(
            functools.partial(local, entries, update_scale, sizes),
            mesh=split_mesh,
            in_specs=(spec, spec),
            out_specs=(spec, spec),
            check_vma=False,
        )(grad, momentum)

    return run
```

```python
import functools
import math

import jax
import jax.numpy as jnp
import numpy as np
from jax import lax
from jax.experimental import pallas as pl
from jax.experimental.pallas import tpu as pltpu
from jax.sharding import Mesh, PartitionSpec as P

ROWS = 576
ITERS = 2

momentum_rate = 0.95
target_rms = 0.5
coef_first = 3.4445
coef_second = -4.775
coef_third = 2.0315

f32, bf16 = jnp.float32, jnp.bfloat16
VMEM = pl.BlockSpec(memory_space=pltpu.VMEM)
SMEM = pl.BlockSpec(memory_space=pltpu.SMEM)
NT = (((1,), (1,)), ((), ()))


def two_sum(a, b):
    s = a + b
    t = s - a
    return s, (a - (s - t)) + (b - t)


def fast_two_sum(a, b):
    s = a + b
    return s, b - (s - a)


def split(a):
    t = 4097.0 * a
    high = t - (t - a)
    return high, a - high


def two_prod(a, b):
    p = a * b
    ah, al = split(a)
    bh, bl = split(b)
    return p, ((ah * bh - p) + ah * bl + al * bh) + al * bl


def dd_add(a, b):
    s, e = two_sum(a[0], b[0])
    return fast_two_sum(s, e + (a[1] + b[1]))


def dd_mul(a, b):
    p, e = two_prod(a[0], b[0])
    return fast_two_sum(p, e + (a[0] * b[1] + a[1] * b[0]))


def dd_const(value):
    high = np.float32(value)
    return float(high), float(np.float32(value - float(high)))


def tree(values):
    while len(values) > 1:
        paired = [dd_add(values[i], values[i + 1]) for i in range(0, len(values) - 1, 2)]
        values = paired + ([values[-1]] if len(values) % 2 else [])
    return values[0]


def fold(a, axis, shifts):
    for shift in shifts:
        a = dd_add(a, (pltpu.roll(a[0], shift, axis), pltpu.roll(a[1], shift, axis)))
    return a


def lanes():
    return lax.broadcasted_iota(jnp.int32, (8, 128), 1)


def pack(values):
    lane = lanes()
    tile = jnp.zeros((8, 128), f32)
    for i, (high, low) in enumerate(values):
        tile = jnp.where(lane == i, high, jnp.where(lane == i + 64, low, tile))
    return tile


def add_rows(ref):
    zero = jnp.zeros((8, 128), f32)
    high, low = fold(tree([(ref[i : i + 8, :], zero) for i in range(0, ref.shape[0], 8)]), 0, (4, 2, 1))
    return fast_two_sum(high, low + pltpu.roll(high, 64, 1))


def sums_kernel(grad_ref, momentum_ref, out_ref, grad_out_ref, momentum_out_ref):
    grad_out_ref[...] = grad_ref[...]
    momentum_out_ref[...] = momentum_ref[...]
    gg, gm, mm = [], [], []
    for i in range(0, grad_ref.shape[1], 8):
        g = grad_ref[0, i : i + 8, :]
        m = momentum_ref[0, i : i + 8, :]
        gg.append(two_prod(g, g))
        gm.append(two_prod(g, m))
        mm.append(two_prod(m, m))
    sums = [fold(fold(tree(v), 0, (4, 2, 1)), 1, (64, 32, 16, 8, 4, 2, 1)) for v in (gg, gm, mm)]
    tile = pack([sums[0]] + sums)
    for i in range(0, out_ref.shape[0], 8):
        out_ref[i : i + 8, :] = tile


def combine_kernel(groups, group_ref, in_ref, out_ref):
    high, low = add_rows(in_ref)
    lane = lanes()
    tile = jnp.where(lane < 64, high, pltpu.roll(low, 64, 1))
    for i in range(0, out_ref.shape[0], 8):
        to = lax.rem(lax.broadcasted_iota(jnp.int32, (8, 128), 0) + i, groups)
        keep = (to == group_ref[0]) | (lax.rem(lane, 64) == 0)
        out_ref[i : i + 8, :] = jnp.where(keep, tile, 0.0)


def scale_kernel(entries, in_ref, grad_ref, momentum_ref, out_ref, own_ref, scale_ref):
    high, low = add_rows(in_ref)
    lane = lanes()

    def value(i):
        return tuple(jnp.sum(jnp.where(lane == i, v, 0.0), axis=1, keepdims=True)[0:1] for v in (high, low))

    square, gg, gm, mm = (value(i) for i in range(4))
    grad_scale = target_rms / (jnp.sqrt(square[0] / entries) + 1e-06)
    rate = float(np.float32(momentum_rate))
    factor_high, factor_low = dd_const(1.0 + rate)
    ones = jnp.ones_like(grad_scale)
    a = two_prod(grad_scale, factor_high * ones)
    a = fast_two_sum(a[0], a[1] + grad_scale * factor_low)
    b = tuple(v * ones for v in dd_const(rate * rate))
    cross = dd_mul(dd_mul((2.0 * a[0], 2.0 * a[1]), b), gm)
    total = dd_add(dd_add(dd_mul(a, dd_mul(a, gg)), dd_mul(dd_mul(b, b), mm)), cross)
    unorm = jnp.sqrt(jnp.maximum(total[0], 0.0))
    scaled_grad = grad_scale * grad_ref[0]
    nudged = scaled_grad + momentum_rate * (momentum_rate * momentum_ref[0] + scaled_grad)
    iterate = (nudged / (unorm + 1e-07)).astype(bf16)
    for i in range(out_ref.shape[0]):
        out_ref[i] = iterate
    own_ref[...] = iterate.astype(f32)
    scale_ref[...] = jnp.broadcast_to(grad_scale, scale_ref.shape)


def transpose_kernel(copies, in_ref, out_ref, flat_ref):
    blocks, rows = in_ref.shape[:2]
    for i in range(blocks):
        flat_ref[i * rows : (i + 1) * rows, :] = in_ref[i].astype(f32)
    half = blocks * rows // 9
    for j in range(9):
        turned = flat_ref[pl.ds(j, half, stride=9), :].T.astype(bf16)
        for i in range(copies):
            if j < 4:
                out_ref[i, 128 * j : 128 * j + 128, 0:half] = turned
            elif j == 4:
                out_ref[i, 512:576, 0:half] = turned[0:64]
                out_ref[i, 0:64, half : 2 * half] = turned[64:128]
            else:
                out_ref[i, 128 * j - 576 : 128 * j - 448, half : 2 * half] = turned


def own_load(flat_ref, pairs):
    low = lax.broadcasted_iota(jnp.int32, (pairs, 128), 1) < 64
    flat = [flat_ref[pl.ds(j, pairs, stride=9), :] for j in range(9)]
    turned = [pltpu.roll(flat[j], 64, 1) for j in range(4, 9)]
    even = flat[:4] + [flat[4]]
    odd = [jnp.where(low, turned[k], turned[k + 1]) for k in range(4)] + [turned[4]]
    return jnp.concatenate([jnp.concatenate(even, 1), jnp.concatenate(odd, 1)], 0)[:, :ROWS]


def own_store(flat_ref, value, pairs):
    value = jnp.concatenate([value, jnp.zeros((2 * pairs, 64), f32)], 1)
    low = lax.broadcasted_iota(jnp.int32, (pairs, 128), 1) < 64
    even = [value[:pairs, 128 * j : 128 * j + 128] for j in range(5)]
    odd = [pltpu.roll(value[pairs:, 128 * j : 128 * j + 128], 64, 1) for j in range(5)]
    flat = even[:4] + [jnp.where(low, even[4], odd[0])]
    flat += [jnp.where(low, odd[k], odd[k + 1]) for k in range(4)]
    for j in range(9):
        flat_ref[pl.ds(j, pairs, stride=9), :] = flat[j]


def gram_kernel(mine_ref, grad_ref, momentum_ref, scale_ref, gram_ref, momentum_out_ref):
    total = None
    for i in range(mine_ref.shape[0]):
        v = mine_ref[i]
        d = lax.dot_general(v, v, NT, preferred_element_type=f32)
        total = d if total is None else total + d
    gram_ref[...] = total
    momentum_out_ref[...] = momentum_rate * momentum_ref[...] + scale_ref[0:1, :] * grad_ref[...]


def iterate_kernel(update_scale, mine_ref, other_ref, gram_ref, own_ref, out_ref, poly_ref, next_ref, flat_ref):
    blocks = [(r, i) for r in (mine_ref, other_ref) for i in range(r.shape[0])]
    pairs = own_ref.shape[0] // 9

    def gram(total, values):
        for get in values:
            v = get()
            d = lax.dot_general(v, v, NT, preferred_element_type=f32)
            total = d if total is None else total + d
        return total

    def poly(gram_matrix):
        low = gram_matrix.astype(bf16)
        squared = jnp.dot(low, low, preferred_element_type=f32)
        return (coef_second * gram_matrix + coef_third * squared).astype(bf16)

    poly_ref[...] = poly(gram(gram_ref[...], [lambda i=i: other_ref[i] for i in range(other_ref.shape[0])]))
    for i, (r, k) in enumerate(blocks):
        v = r[k]
        product = jnp.dot(poly_ref[...], v, preferred_element_type=f32)
        next_ref[i] = (coef_first * v.astype(f32) + product).astype(bf16)
    own = own_load(own_ref, pairs)
    product = jnp.dot(own.astype(bf16), poly_ref[...], preferred_element_type=f32)
    own = (coef_first * own + product).astype(bf16)
    poly_ref[...] = poly(gram(None, [lambda i=i: next_ref[i] for i in range(len(blocks))]))
    product = jnp.dot(own, poly_ref[...], preferred_element_type=f32)
    own_store(flat_ref, update_scale * (coef_first * own.astype(f32) + product), pairs)
    out_ref[0] = flat_ref[...].astype(bf16)


def kernel(body, name, out, in_specs, scratch=(), cost=None):
    return pl.pallas_call(
        body,
        name=name,
        out_shape=out,
        in_specs=in_specs,
        out_specs=jax.tree.map(lambda _: VMEM, out),
        scratch_shapes=list(scratch),
        compiler_params=pltpu.CompilerParams(vmem_limit_bytes=40 * 2**20),
        cost_estimate=cost,
    )


def local(entries, update_scale, sizes, grad, momentum):
    nx, ny, nc, ng = sizes
    rows = grad.shape[1]
    columns = ny * rows * 128 // ROWS
    shape = jax.ShapeDtypeStruct
    group = lax.axis_index("group").astype(jnp.int32).reshape(1)
    grad, momentum, group = lax.optimization_barrier((grad, momentum, group))
    sums, grad, momentum = kernel(
        sums_kernel,
        "sums",
        (shape((nx * ny, 128), f32), shape(grad.shape, f32), shape(grad.shape, f32)),
        [VMEM] * 2,
    )(grad, momentum)
    sums = lax.all_to_all(sums.reshape(-1, 1, 128), ("x", "y"), 0, 0).reshape(-1, 128)
    sums = kernel(functools.partial(combine_kernel, ng), "combine", shape((nc * ng, 128), f32), [SMEM, VMEM])(group, sums)
    sums = lax.all_to_all(sums.reshape(-1, 1, 128), ("core", "group"), 0, 0).reshape(-1, 128)
    iterate, own, scale = kernel(
        functools.partial(scale_kernel, entries),
        "scale",
        (shape((ny, rows, 128), bf16), shape((rows, 128), f32), shape((8, 128), f32)),
        [VMEM] * 3,
    )(sums, grad, momentum)
    gathered = lax.all_to_all(iterate, "y", 0, 0)
    turned = kernel(
        functools.partial(transpose_kernel, nx),
        "turn",
        shape((nx, ROWS, columns), bf16),
        [VMEM],
        scratch=[pltpu.VMEM((ny * rows, 128), f32)],
    )(gathered)
    mine = lax.all_to_all(turned, "x", 0, 0)
    other = lax.ppermute(mine, "core", [(0, 1), (1, 0)])
    gram, momentum_out = kernel(
        gram_kernel,
        "gram",
        (shape((ROWS, ROWS), f32), shape(grad.shape, f32)),
        [VMEM] * 4,
        cost=pl.CostEstimate(flops=2 * ROWS * ROWS * columns * nx, bytes_accessed=2 * ROWS * columns * nx, transcendentals=0),
    )(mine, grad, momentum, scale)
    update = kernel(
        functools.partial(iterate_kernel, update_scale),
        "newton",
        shape(grad.shape, bf16),
        [VMEM] * 4,
        scratch=[
            pltpu.VMEM((ROWS, ROWS), bf16),
            pltpu.VMEM((2 * nx, ROWS, columns), bf16),
            pltpu.VMEM((rows, 128), f32),
        ],
    )(mine, other, gram, own)
    return momentum_out, update


def solution(mesh):
    sizes = (4, 8, 2, 12)
    split_mesh = Mesh(mesh.devices.reshape(sizes), ("x", "y", "core", "group"))
    spec = P("group", ("x", "y", "core"), None)

    def run(grad, momentum):
        entries = grad.size
        layers, flat_rows, _ = grad.shape
        width = flat_rows * 128 // ROWS
        update_scale = 0.2 * math.sqrt(max(ROWS, width))
        return jax.shard_map(
            functools.partial(local, entries, update_scale, sizes),
            mesh=split_mesh,
            in_specs=(spec, spec),
            out_specs=(spec, spec),
            check_vma=False,
        )(grad, momentum)

    return run
```

```python
import functools
import math

import jax
import jax.numpy as jnp
import numpy as np
from jax import lax
from jax.experimental import pallas as pl
from jax.experimental.pallas import tpu as pltpu
from jax.sharding import Mesh, PartitionSpec as P

ROWS = 576
ITERS = 2

momentum_rate = 0.95
target_rms = 0.5
coef_first = 3.4445
coef_second = -4.775
coef_third = 2.0315

f32, bf16 = jnp.float32, jnp.bfloat16
VMEM = pl.BlockSpec(memory_space=pltpu.VMEM)
SMEM = pl.BlockSpec(memory_space=pltpu.SMEM)
NT = (((1,), (1,)), ((), ()))


def two_sum(a, b):
    s = a + b
    t = s - a
    return s, (a - (s - t)) + (b - t)


def fast_two_sum(a, b):
    s = a + b
    return s, b - (s - a)


def split(a):
    t = 4097.0 * a
    high = t - (t - a)
    return high, a - high


def two_prod(a, b):
    p = a * b
    ah, al = split(a)
    bh, bl = split(b)
    return p, ((ah * bh - p) + ah * bl + al * bh) + al * bl


def dd_add(a, b):
    s, e = two_sum(a[0], b[0])
    return fast_two_sum(s, e + (a[1] + b[1]))


def dd_mul(a, b):
    p, e = two_prod(a[0], b[0])
    return fast_two_sum(p, e + (a[0] * b[1] + a[1] * b[0]))


def dd_const(value):
    high = np.float32(value)
    return float(high), float(np.float32(value - float(high)))


def tree(values):
    while len(values) > 1:
        paired = [dd_add(values[i], values[i + 1]) for i in range(0, len(values) - 1, 2)]
        values = paired + ([values[-1]] if len(values) % 2 else [])
    return values[0]


def fold(a, axis, shifts):
    for shift in shifts:
        a = dd_add(a, (pltpu.roll(a[0], shift, axis), pltpu.roll(a[1], shift, axis)))
    return a


def lanes():
    return lax.broadcasted_iota(jnp.int32, (8, 128), 1)


def pack(values):
    lane = lanes()
    tile = jnp.zeros((8, 128), f32)
    for i, (high, low) in enumerate(values):
        tile = jnp.where(lane == i, high, jnp.where(lane == i + 64, low, tile))
    return tile


def add_rows(ref):
    zero = jnp.zeros((8, 128), f32)
    high, low = fold(tree([(ref[i : i + 8, :], zero) for i in range(0, ref.shape[0], 8)]), 0, (4, 2, 1))
    return fast_two_sum(high, low + pltpu.roll(high, 64, 1))


def sums_kernel(pair_ref, out_ref):
    gg, gm, mm = [], [], []
    for i in range(0, pair_ref.shape[1], 8):
        g = pair_ref[0, i : i + 8, :]
        m = pair_ref[1, i : i + 8, :]
        gg.append(two_prod(g, g))
        gm.append(two_prod(g, m))
        mm.append(two_prod(m, m))
    sums = [fold(fold(tree(v), 0, (4, 2, 1)), 1, (64, 32, 16, 8, 4, 2, 1)) for v in (gg, gm, mm)]
    tile = pack([sums[0]] + sums)
    for i in range(0, out_ref.shape[0], 8):
        out_ref[i : i + 8, :] = tile


def combine_kernel(groups, group_ref, in_ref, out_ref):
    high, low = add_rows(in_ref)
    lane = lanes()
    tile = jnp.where(lane < 64, high, pltpu.roll(low, 64, 1))
    for i in range(0, out_ref.shape[0], 8):
        to = lax.rem(lax.broadcasted_iota(jnp.int32, (8, 128), 0) + i, groups)
        keep = (to == group_ref[0]) | (lax.rem(lane, 64) == 0)
        out_ref[i : i + 8, :] = jnp.where(keep, tile, 0.0)


def scale_kernel(entries, in_ref, pair_ref, out_ref, own_ref, scale_ref):
    high, low = add_rows(in_ref)
    lane = lanes()

    def value(i):
        return tuple(jnp.sum(jnp.where(lane == i, v, 0.0), axis=1, keepdims=True)[0:1] for v in (high, low))

    square, gg, gm, mm = (value(i) for i in range(4))
    grad_scale = target_rms / (jnp.sqrt(square[0] / entries) + 1e-06)
    rate = float(np.float32(momentum_rate))
    factor_high, factor_low = dd_const(1.0 + rate)
    ones = jnp.ones_like(grad_scale)
    a = two_prod(grad_scale, factor_high * ones)
    a = fast_two_sum(a[0], a[1] + grad_scale * factor_low)
    b = tuple(v * ones for v in dd_const(rate * rate))
    cross = dd_mul(dd_mul((2.0 * a[0], 2.0 * a[1]), b), gm)
    total = dd_add(dd_add(dd_mul(a, dd_mul(a, gg)), dd_mul(dd_mul(b, b), mm)), cross)
    unorm = jnp.sqrt(jnp.maximum(total[0], 0.0))
    scaled_grad = grad_scale * pair_ref[0]
    nudged = scaled_grad + momentum_rate * (momentum_rate * pair_ref[1] + scaled_grad)
    iterate = (nudged / (unorm + 1e-07)).astype(bf16)
    for i in range(out_ref.shape[0]):
        out_ref[i] = iterate
    own_ref[...] = iterate.astype(f32)
    scale_ref[...] = jnp.broadcast_to(grad_scale, scale_ref.shape)


def transpose_kernel(copies, in_ref, out_ref, flat_ref):
    blocks, rows = in_ref.shape[:2]
    for i in range(blocks):
        flat_ref[i * rows : (i + 1) * rows, :] = in_ref[i].astype(f32)
    half = blocks * rows // 9
    for j in range(9):
        turned = flat_ref[pl.ds(j, half, stride=9), :].T.astype(bf16)
        for i in range(copies):
            if j < 4:
                out_ref[i, 128 * j : 128 * j + 128, 0:half] = turned
            elif j == 4:
                out_ref[i, 512:576, 0:half] = turned[0:64]
                out_ref[i, 0:64, half : 2 * half] = turned[64:128]
            else:
                out_ref[i, 128 * j - 576 : 128 * j - 448, half : 2 * half] = turned


def own_load(flat_ref, pairs):
    low = lax.broadcasted_iota(jnp.int32, (pairs, 128), 1) < 64
    flat = [flat_ref[pl.ds(j, pairs, stride=9), :] for j in range(9)]
    turned = [pltpu.roll(flat[j], 64, 1) for j in range(4, 9)]
    even = flat[:4] + [flat[4]]
    odd = [jnp.where(low, turned[k], turned[k + 1]) for k in range(4)] + [turned[4]]
    return jnp.concatenate([jnp.concatenate(even, 1), jnp.concatenate(odd, 1)], 0)[:, :ROWS]


def own_store(flat_ref, value, pairs):
    value = jnp.concatenate([value, jnp.zeros((2 * pairs, 64), f32)], 1)
    low = lax.broadcasted_iota(jnp.int32, (pairs, 128), 1) < 64
    even = [value[:pairs, 128 * j : 128 * j + 128] for j in range(5)]
    odd = [pltpu.roll(value[pairs:, 128 * j : 128 * j + 128], 64, 1) for j in range(5)]
    flat = even[:4] + [jnp.where(low, even[4], odd[0])]
    flat += [jnp.where(low, odd[k], odd[k + 1]) for k in range(4)]
    for j in range(9):
        flat_ref[pl.ds(j, pairs, stride=9), :] = flat[j]


def triangle():
    return [(a, min(a + 256, ROWS)) for a in range(0, ROWS, 256)]


def side_by_side(values):
    return jnp.concatenate(values, 1)


def gram_columns(iterate):
    return [lax.dot_general(iterate[a:], iterate[a:b], NT, preferred_element_type=f32) for a, b in triangle()]


def mirror(ref, value, a, b):
    ref[a:, a:b] = value
    if b < ROWS:
        ref[a:b, b:] = value[b - a :].T


def store_poly(columns, low_ref, poly_ref):
    for (a, b), column in zip(triangle(), columns):
        mirror(low_ref, column.astype(bf16), a, b)
    for (a, b), column in zip(triangle(), columns):
        squared = jnp.dot(low_ref[a:, :], low_ref[:, a:b], preferred_element_type=f32)
        mirror(poly_ref, (coef_second * column + coef_third * squared).astype(bf16), a, b)


def gram_kernel(mine_ref, pair_ref, scale_ref, gram_ref, momentum_out_ref):
    iterate = side_by_side([mine_ref[i] for i in range(mine_ref.shape[0])])
    for (a, b), column in zip(triangle(), gram_columns(iterate)):
        gram_ref[a:, a:b] = column
    momentum_out_ref[0] = momentum_rate * pair_ref[1] + scale_ref[0:1, :] * pair_ref[0]


def iterate_kernel(update_scale, mine_ref, other_ref, gram_ref, own_ref, out_ref, poly_ref, next_ref, flat_ref, low_ref):
    blocks = [(r, i) for r in (mine_ref, other_ref) for i in range(r.shape[0])]
    pairs = own_ref.shape[0] // 9
    columns = gram_columns(side_by_side([other_ref[i] for i in range(other_ref.shape[0])]))
    columns = [gram_ref[a:, a:b] + column for (a, b), column in zip(triangle(), columns)]
    store_poly(columns, low_ref, poly_ref)
    for i, (r, k) in enumerate(blocks):
        v = r[k]
        product = jnp.dot(poly_ref[...], v, preferred_element_type=f32)
        next_ref[i] = (coef_first * v.astype(f32) + product).astype(bf16)
    own = own_load(own_ref, pairs)
    product = jnp.dot(own.astype(bf16), poly_ref[...], preferred_element_type=f32)
    own = (coef_first * own + product).astype(bf16)
    store_poly(gram_columns(side_by_side([next_ref[i] for i in range(len(blocks))])), low_ref, poly_ref)
    product = jnp.dot(own, poly_ref[...], preferred_element_type=f32)
    own_store(flat_ref, update_scale * (coef_first * own.astype(f32) + product), pairs)
    out_ref[0] = flat_ref[...].astype(bf16)


def kernel(body, name, out, in_specs, scratch=(), cost=None):
    return pl.pallas_call(
        body,
        name=name,
        out_shape=out,
        in_specs=in_specs,
        out_specs=jax.tree.map(lambda _: VMEM, out),
        scratch_shapes=list(scratch),
        compiler_params=pltpu.CompilerParams(vmem_limit_bytes=40 * 2**20),
        cost_estimate=cost,
    )


def local(entries, update_scale, sizes, grad, momentum):
    nx, ny, nc, ng = sizes
    rows = grad.shape[1]
    columns = ny * rows * 128 // ROWS
    shape = jax.ShapeDtypeStruct
    group = lax.axis_index("group").astype(jnp.int32).reshape(1)
    grad, momentum, group = lax.optimization_barrier((grad, momentum, group))
    first = lax.broadcasted_iota(jnp.int32, (2, rows, 128), 0) == 0
    pair = jnp.where(first, grad, momentum)
    sums = kernel(sums_kernel, "sums", shape((ny * nc, 128), f32), [VMEM])(pair)
    sums = lax.all_to_all(sums.reshape(-1, 1, 128), ("y", "core"), 0, 0).reshape(-1, 128)
    sums = kernel(functools.partial(combine_kernel, ng), "combine", shape((nx * ng, 128), f32), [SMEM, VMEM])(group, sums)
    sums = lax.all_to_all(sums.reshape(-1, 1, 128), ("x", "group"), 0, 0).reshape(-1, 128)
    iterate, own, scale = kernel(
        functools.partial(scale_kernel, entries),
        "scale",
        (shape((ny, rows, 128), bf16), shape((rows, 128), f32), shape((8, 128), f32)),
        [VMEM] * 2,
    )(sums, pair)
    gathered = lax.all_to_all(iterate, "y", 0, 0)
    turned = kernel(
        functools.partial(transpose_kernel, nx),
        "turn",
        shape((nx, ROWS, columns), bf16),
        [VMEM],
        scratch=[pltpu.VMEM((ny * rows, 128), f32)],
    )(gathered)
    mine = lax.all_to_all(turned, "x", 0, 0)
    other = lax.ppermute(mine, "core", [(0, 1), (1, 0)])
    gram, momentum_out = kernel(
        gram_kernel,
        "gram",
        (shape((ROWS, ROWS), f32), shape(grad.shape, f32)),
        [VMEM] * 3,
        cost=pl.CostEstimate(flops=2 * ROWS * ROWS * columns * nx, bytes_accessed=2 * ROWS * columns * nx, transcendentals=0),
    )(mine, pair, scale)
    update = kernel(
        functools.partial(iterate_kernel, update_scale),
        "newton",
        shape(grad.shape, bf16),
        [VMEM] * 4,
        scratch=[
            pltpu.VMEM((ROWS, ROWS), bf16),
            pltpu.VMEM((2 * nx, ROWS, columns), bf16),
            pltpu.VMEM((rows, 128), f32),
            pltpu.VMEM((ROWS, ROWS), bf16),
        ],
    )(mine, other, gram, own)
    return momentum_out, update


def solution(mesh):
    sizes = (4, 8, 2, 12)
    split_mesh = Mesh(mesh.devices.reshape(sizes), ("x", "y", "core", "group"))
    spec = P("group", ("x", "y", "core"), None)

    def run(grad, momentum):
        entries = grad.size
        layers, flat_rows, _ = grad.shape
        width = flat_rows * 128 // ROWS
        update_scale = 0.2 * math.sqrt(max(ROWS, width))
        return jax.shard_map(
            functools.partial(local, entries, update_scale, sizes),
            mesh=split_mesh,
            in_specs=(spec, spec),
            out_specs=(spec, spec),
            check_vma=False,
        )(grad, momentum)

    return run
```

```python
import functools
import math

import jax
import jax.numpy as jnp
import numpy as np
from jax import lax
from jax.experimental import pallas as pl
from jax.experimental.pallas import tpu as pltpu
from jax.sharding import Mesh, PartitionSpec as P

ROWS = 576
ITERS = 2

momentum_rate = 0.95
target_rms = 0.5
coef_first = 3.4445
coef_second = -4.775
coef_third = 2.0315

f32, bf16 = jnp.float32, jnp.bfloat16
VMEM = pl.BlockSpec(memory_space=pltpu.VMEM)
SMEM = pl.BlockSpec(memory_space=pltpu.SMEM)
NT = (((1,), (1,)), ((), ()))


def two_sum(a, b):
    s = a + b
    t = s - a
    return s, (a - (s - t)) + (b - t)


def fast_two_sum(a, b):
    s = a + b
    return s, b - (s - a)


def split(a):
    t = 4097.0 * a
    high = t - (t - a)
    return high, a - high


def two_prod(a, b):
    p = a * b
    ah, al = split(a)
    bh, bl = split(b)
    return p, ((ah * bh - p) + ah * bl + al * bh) + al * bl


def dd_add(a, b):
    s, e = two_sum(a[0], b[0])
    return fast_two_sum(s, e + (a[1] + b[1]))


def dd_mul(a, b):
    p, e = two_prod(a[0], b[0])
    return fast_two_sum(p, e + (a[0] * b[1] + a[1] * b[0]))


def dd_const(value):
    high = np.float32(value)
    return float(high), float(np.float32(value - float(high)))


def tree(values):
    while len(values) > 1:
        paired = [dd_add(values[i], values[i + 1]) for i in range(0, len(values) - 1, 2)]
        values = paired + ([values[-1]] if len(values) % 2 else [])
    return values[0]


def fold(a, axis, shifts):
    for shift in shifts:
        a = dd_add(a, (pltpu.roll(a[0], shift, axis), pltpu.roll(a[1], shift, axis)))
    return a


def lanes():
    return lax.broadcasted_iota(jnp.int32, (8, 128), 1)


def pack(values):
    lane = lanes()
    tile = jnp.zeros((8, 128), f32)
    for i, (high, low) in enumerate(values):
        tile = jnp.where(lane == i, high, jnp.where(lane == i + 64, low, tile))
    return tile


def add_rows(ref):
    zero = jnp.zeros((8, 128), f32)
    high, low = fold(tree([(ref[i : i + 8, :], zero) for i in range(0, ref.shape[0], 8)]), 0, (4, 2, 1))
    return fast_two_sum(high, low + pltpu.roll(high, 64, 1))


def sums_kernel(pair_ref, out_ref):
    gg, gm, mm = [], [], []
    for i in range(0, pair_ref.shape[1], 8):
        g = pair_ref[0, i : i + 8, :]
        m = pair_ref[1, i : i + 8, :]
        gg.append(two_prod(g, g))
        gm.append(two_prod(g, m))
        mm.append(two_prod(m, m))
    sums = [fold(fold(tree(v), 0, (4, 2, 1)), 1, (64, 32, 16, 8, 4, 2, 1)) for v in (gg, gm, mm)]
    tile = pack([sums[0]] + sums)
    for i in range(0, out_ref.shape[0], 8):
        out_ref[i : i + 8, :] = tile


def combine_kernel(groups, group_ref, in_ref, out_ref):
    high, low = add_rows(in_ref)
    lane = lanes()
    tile = jnp.where(lane < 64, high, pltpu.roll(low, 64, 1))
    for i in range(0, out_ref.shape[0], 8):
        to = lax.rem(lax.broadcasted_iota(jnp.int32, (8, 128), 0) + i, groups)
        keep = (to == group_ref[0]) | (lax.rem(lane, 64) == 0)
        out_ref[i : i + 8, :] = jnp.where(keep, tile, 0.0)


def scale_kernel(entries, in_ref, pair_ref, out_ref, own_ref, scale_ref):
    high, low = add_rows(in_ref)
    lane = lanes()

    def value(i):
        return tuple(jnp.sum(jnp.where(lane == i, v, 0.0), axis=1, keepdims=True)[0:1] for v in (high, low))

    square, gg, gm, mm = (value(i) for i in range(4))
    grad_scale = target_rms / (jnp.sqrt(square[0] / entries) + 1e-06)
    rate = float(np.float32(momentum_rate))
    factor_high, factor_low = dd_const(1.0 + rate)
    ones = jnp.ones_like(grad_scale)
    a = two_prod(grad_scale, factor_high * ones)
    a = fast_two_sum(a[0], a[1] + grad_scale * factor_low)
    b = tuple(v * ones for v in dd_const(rate * rate))
    cross = dd_mul(dd_mul((2.0 * a[0], 2.0 * a[1]), b), gm)
    total = dd_add(dd_add(dd_mul(a, dd_mul(a, gg)), dd_mul(dd_mul(b, b), mm)), cross)
    unorm = jnp.sqrt(jnp.maximum(total[0], 0.0))
    scaled_grad = grad_scale * pair_ref[0]
    nudged = scaled_grad + momentum_rate * (momentum_rate * pair_ref[1] + scaled_grad)
    iterate = (nudged / (unorm + 1e-07)).astype(bf16)
    for i in range(out_ref.shape[0]):
        out_ref[i] = iterate
    own_ref[...] = iterate.astype(f32)
    scale_ref[...] = jnp.broadcast_to(grad_scale, scale_ref.shape)


def transpose_kernel(copies, in_ref, out_ref, flat_ref):
    blocks, rows = in_ref.shape[:2]
    for i in range(blocks):
        flat_ref[i * rows : (i + 1) * rows, :] = in_ref[i].astype(f32)
    half = blocks * rows // 9
    for j in range(9):
        turned = flat_ref[pl.ds(j, half, stride=9), :].T.astype(bf16)
        for i in range(copies):
            if j < 4:
                out_ref[i, 128 * j : 128 * j + 128, 0:half] = turned
            elif j == 4:
                out_ref[i, 512:576, 0:half] = turned[0:64]
                out_ref[i, 0:64, half : 2 * half] = turned[64:128]
            else:
                out_ref[i, 128 * j - 576 : 128 * j - 448, half : 2 * half] = turned


def own_load(flat_ref, pairs):
    low = lax.broadcasted_iota(jnp.int32, (pairs, 128), 1) < 64
    flat = [flat_ref[pl.ds(j, pairs, stride=9), :] for j in range(9)]
    turned = [pltpu.roll(flat[j], 64, 1) for j in range(4, 9)]
    even = flat[:4] + [flat[4]]
    odd = [jnp.where(low, turned[k], turned[k + 1]) for k in range(4)] + [turned[4]]
    return jnp.concatenate([jnp.concatenate(even, 1), jnp.concatenate(odd, 1)], 0)[:, :ROWS]


def own_store(flat_ref, value, pairs):
    value = jnp.concatenate([value, jnp.zeros((2 * pairs, 64), f32)], 1)
    low = lax.broadcasted_iota(jnp.int32, (pairs, 128), 1) < 64
    even = [value[:pairs, 128 * j : 128 * j + 128] for j in range(5)]
    odd = [pltpu.roll(value[pairs:, 128 * j : 128 * j + 128], 64, 1) for j in range(5)]
    flat = even[:4] + [jnp.where(low, even[4], odd[0])]
    flat += [jnp.where(low, odd[k], odd[k + 1]) for k in range(4)]
    for j in range(9):
        flat_ref[pl.ds(j, pairs, stride=9), :] = flat[j]


def triangle():
    return [(a, min(a + 256, ROWS)) for a in range(0, ROWS, 256)]


def side_by_side(values):
    return jnp.concatenate(values, 1)


def gram_columns(iterate):
    return [lax.dot_general(iterate[a:], iterate[a:b], NT, preferred_element_type=f32) for a, b in triangle()]


def mirror(ref, value, a, b):
    ref[a:, a:b] = value
    if b < ROWS:
        ref[a:b, b:] = value[b - a :].T


def store_poly(columns, low_ref, poly_ref):
    for (a, b), column in zip(triangle(), columns):
        mirror(low_ref, column.astype(bf16), a, b)
    for (a, b), column in zip(triangle(), columns):
        squared = jnp.dot(low_ref[a:, :], low_ref[:, a:b], preferred_element_type=f32)
        mirror(poly_ref, (coef_second * column + coef_third * squared).astype(bf16), a, b)


def gram_kernel(mine_ref, pair_ref, scale_ref, gram_ref, momentum_out_ref):
    iterate = side_by_side([mine_ref[i] for i in range(mine_ref.shape[0])])
    for (a, b), column in zip(triangle(), gram_columns(iterate)):
        gram_ref[a:, a:b] = column
    momentum_out_ref[0] = momentum_rate * pair_ref[1] + scale_ref[0:1, :] * pair_ref[0]


def iterate_kernel(update_scale, mine_ref, other_ref, gram_ref, own_ref, out_ref, poly_ref, next_ref, flat_ref, low_ref):
    blocks = [side_by_side([r[i], r[i + 1]]) for r in (mine_ref, other_ref) for i in range(0, r.shape[0], 2)]
    pairs = own_ref.shape[0] // 9
    columns = gram_columns(side_by_side([other_ref[i] for i in range(other_ref.shape[0])]))
    columns = [gram_ref[a:, a:b] + column for (a, b), column in zip(triangle(), columns)]
    store_poly(columns, low_ref, poly_ref)
    for i, v in enumerate(blocks):
        product = jnp.dot(poly_ref[...], v, preferred_element_type=f32)
        next_ref[i] = (coef_first * v.astype(f32) + product).astype(bf16)
    own = own_load(own_ref, pairs)
    product = jnp.dot(own.astype(bf16), poly_ref[...], preferred_element_type=f32)
    own = (coef_first * own + product).astype(bf16)
    store_poly(gram_columns(side_by_side([next_ref[i] for i in range(len(blocks))])), low_ref, poly_ref)
    product = jnp.dot(own, poly_ref[...], preferred_element_type=f32)
    own_store(flat_ref, update_scale * (coef_first * own.astype(f32) + product), pairs)
    out_ref[0] = flat_ref[...].astype(bf16)


def kernel(body, name, out, in_specs, scratch=(), cost=None):
    return pl.pallas_call(
        body,
        name=name,
        out_shape=out,
        in_specs=in_specs,
        out_specs=jax.tree.map(lambda _: VMEM, out),
        scratch_shapes=list(scratch),
        compiler_params=pltpu.CompilerParams(vmem_limit_bytes=40 * 2**20),
        cost_estimate=cost,
    )


def local(entries, update_scale, sizes, grad, momentum):
    nx, nh, nl, nc, ng = sizes
    rows = grad.shape[1]
    columns = nh * rows * 128 // ROWS
    copies = nx * nl
    shape = jax.ShapeDtypeStruct
    group = lax.axis_index("group").astype(jnp.int32).reshape(1)
    grad, momentum, group = lax.optimization_barrier((grad, momentum, group))
    first = lax.broadcasted_iota(jnp.int32, (2, rows, 128), 0) == 0
    pair = jnp.where(first, grad, momentum)
    sums = kernel(sums_kernel, "sums", shape((nh * nl * nc, 128), f32), [VMEM])(pair)
    sums = lax.all_to_all(sums.reshape(-1, 1, 128), ("yh", "yl", "core"), 0, 0).reshape(-1, 128)
    sums = kernel(functools.partial(combine_kernel, ng), "combine", shape((nx * ng, 128), f32), [SMEM, VMEM])(group, sums)
    sums = lax.all_to_all(sums.reshape(-1, 1, 128), ("x", "group"), 0, 0).reshape(-1, 128)
    iterate, own, scale = kernel(
        functools.partial(scale_kernel, entries),
        "scale",
        (shape((nh, rows, 128), bf16), shape((rows, 128), f32), shape((8, 128), f32)),
        [VMEM] * 2,
    )(sums, pair)
    gathered = lax.all_to_all(iterate, "yh", 0, 0)
    turned = kernel(
        functools.partial(transpose_kernel, copies),
        "turn",
        shape((copies, ROWS, columns), bf16),
        [VMEM],
        scratch=[pltpu.VMEM((nh * rows, 128), f32)],
    )(gathered)
    mine = lax.all_to_all(turned, ("x", "yl"), 0, 0)
    other = lax.ppermute(mine, "core", [(0, 1), (1, 0)])
    gram, momentum_out = kernel(
        gram_kernel,
        "gram",
        (shape((ROWS, ROWS), f32), shape(grad.shape, f32)),
        [VMEM] * 3,
        cost=pl.CostEstimate(flops=2 * ROWS * ROWS * columns * copies, bytes_accessed=2 * ROWS * columns * copies, transcendentals=0),
    )(mine, pair, scale)
    update = kernel(
        functools.partial(iterate_kernel, update_scale),
        "newton",
        shape(grad.shape, bf16),
        [VMEM] * 4,
        scratch=[
            pltpu.VMEM((ROWS, ROWS), bf16),
            pltpu.VMEM((copies, ROWS, 2 * columns), bf16),
            pltpu.VMEM((rows, 128), f32),
            pltpu.VMEM((ROWS, ROWS), bf16),
        ],
    )(mine, other, gram, own)
    return momentum_out, update


def solution(mesh):
    sizes = (4, 4, 2, 2, 12)
    split_mesh = Mesh(mesh.devices.reshape(sizes), ("x", "yh", "yl", "core", "group"))
    spec = P("group", ("x", "yh", "yl", "core"), None)

    def run(grad, momentum):
        entries = grad.size
        layers, flat_rows, _ = grad.shape
        width = flat_rows * 128 // ROWS
        update_scale = 0.2 * math.sqrt(max(ROWS, width))
        return jax.shard_map(
            functools.partial(local, entries, update_scale, sizes),
            mesh=split_mesh,
            in_specs=(spec, spec),
            out_specs=(spec, spec),
            check_vma=False,
        )(grad, momentum)

    return run
```

```python
import functools
import math

import jax
import jax.numpy as jnp
import numpy as np
from jax import lax
from jax.experimental import pallas as pl
from jax.experimental.pallas import tpu as pltpu
from jax.sharding import Mesh, PartitionSpec as P

ROWS = 576
ITERS = 2

momentum_rate = 0.95
target_rms = 0.5
coef_first = 3.4445
coef_second = -4.775
coef_third = 2.0315

f32, bf16 = jnp.float32, jnp.bfloat16
VMEM = pl.BlockSpec(memory_space=pltpu.VMEM)
SMEM = pl.BlockSpec(memory_space=pltpu.SMEM)
NT = (((1,), (1,)), ((), ()))


def two_sum(a, b):
    s = a + b
    t = s - a
    return s, (a - (s - t)) + (b - t)


def fast_two_sum(a, b):
    s = a + b
    return s, b - (s - a)


def split(a):
    t = 4097.0 * a
    high = t - (t - a)
    return high, a - high


def two_prod(a, b):
    p = a * b
    ah, al = split(a)
    bh, bl = split(b)
    return p, ((ah * bh - p) + ah * bl + al * bh) + al * bl


def dd_add(a, b):
    s, e = two_sum(a[0], b[0])
    return fast_two_sum(s, e + (a[1] + b[1]))


def dd_mul(a, b):
    p, e = two_prod(a[0], b[0])
    return fast_two_sum(p, e + (a[0] * b[1] + a[1] * b[0]))


def dd_const(value):
    high = np.float32(value)
    return float(high), float(np.float32(value - float(high)))


def tree(values):
    while len(values) > 1:
        paired = [dd_add(values[i], values[i + 1]) for i in range(0, len(values) - 1, 2)]
        values = paired + ([values[-1]] if len(values) % 2 else [])
    return values[0]


def fold(a, axis, shifts):
    for shift in shifts:
        a = dd_add(a, (pltpu.roll(a[0], shift, axis), pltpu.roll(a[1], shift, axis)))
    return a


def lanes():
    return lax.broadcasted_iota(jnp.int32, (8, 128), 1)


def pack(values):
    lane = lanes()
    tile = jnp.zeros((8, 128), f32)
    for i, (high, low) in enumerate(values):
        tile = jnp.where(lane == i, high, jnp.where(lane == i + 64, low, tile))
    return tile


def add_rows(ref):
    zero = jnp.zeros((8, 128), f32)
    high, low = fold(tree([(ref[i : i + 8, :], zero) for i in range(0, ref.shape[0], 8)]), 0, (4, 2, 1))
    return fast_two_sum(high, low + pltpu.roll(high, 64, 1))


def sums_kernel(pair_ref, out_ref):
    gg, gm, mm = [], [], []
    for i in range(0, pair_ref.shape[1], 8):
        g = pair_ref[0, i : i + 8, :]
        m = pair_ref[1, i : i + 8, :]
        gg.append(two_prod(g, g))
        gm.append(two_prod(g, m))
        mm.append(two_prod(m, m))
    sums = [fold(fold(tree(v), 0, (4, 2, 1)), 1, (64, 32, 16, 8, 4, 2, 1)) for v in (gg, gm, mm)]
    tile = pack([sums[0]] + sums)
    for i in range(0, out_ref.shape[0], 8):
        out_ref[i : i + 8, :] = tile


def combine_kernel(groups, group_ref, in_ref, out_ref):
    high, low = add_rows(in_ref)
    lane = lanes()
    tile = jnp.where(lane < 64, high, pltpu.roll(low, 64, 1))
    for i in range(0, out_ref.shape[0], 8):
        to = lax.rem(lax.broadcasted_iota(jnp.int32, (8, 128), 0) + i, groups)
        keep = (to == group_ref[0]) | (lax.rem(lane, 64) == 0)
        out_ref[i : i + 8, :] = jnp.where(keep, tile, 0.0)


def scale_kernel(entries, in_ref, pair_ref, out_ref, own_ref, scale_ref):
    high, low = add_rows(in_ref)
    lane = lanes()

    def value(i):
        return tuple(jnp.sum(jnp.where(lane == i, v, 0.0), axis=1, keepdims=True)[0:1] for v in (high, low))

    square, gg, gm, mm = (value(i) for i in range(4))
    grad_scale = target_rms / (jnp.sqrt(square[0] / entries) + 1e-06)
    rate = float(np.float32(momentum_rate))
    factor_high, factor_low = dd_const(1.0 + rate)
    ones = jnp.ones_like(grad_scale)
    a = two_prod(grad_scale, factor_high * ones)
    a = fast_two_sum(a[0], a[1] + grad_scale * factor_low)
    b = tuple(v * ones for v in dd_const(rate * rate))
    cross = dd_mul(dd_mul((2.0 * a[0], 2.0 * a[1]), b), gm)
    total = dd_add(dd_add(dd_mul(a, dd_mul(a, gg)), dd_mul(dd_mul(b, b), mm)), cross)
    unorm = jnp.sqrt(jnp.maximum(total[0], 0.0))
    scaled_grad = grad_scale * pair_ref[0]
    nudged = scaled_grad + momentum_rate * (momentum_rate * pair_ref[1] + scaled_grad)
    iterate = (nudged / (unorm + 1e-07)).astype(bf16)
    for i in range(out_ref.shape[0]):
        out_ref[i] = iterate
    own_ref[...] = iterate.astype(f32)
    scale_ref[...] = jnp.broadcast_to(grad_scale, scale_ref.shape)


def transpose_kernel(copies, in_ref, out_ref, flat_ref):
    blocks, rows = in_ref.shape[:2]
    for i in range(blocks):
        flat_ref[i * rows : (i + 1) * rows, :] = in_ref[i].astype(f32)
    half = blocks * rows // 9
    for j in range(9):
        turned = flat_ref[pl.ds(j, half, stride=9), :].T.astype(bf16)
        for i in range(copies):
            if j < 4:
                out_ref[i, 128 * j : 128 * j + 128, 0:half] = turned
            elif j == 4:
                out_ref[i, 512:576, 0:half] = turned[0:64]
                out_ref[i, 0:64, half : 2 * half] = turned[64:128]
            else:
                out_ref[i, 128 * j - 576 : 128 * j - 448, half : 2 * half] = turned


def own_load(flat_ref, pairs):
    low = lax.broadcasted_iota(jnp.int32, (pairs, 128), 1) < 64
    flat = [flat_ref[pl.ds(j, pairs, stride=9), :] for j in range(9)]
    turned = [pltpu.roll(flat[j], 64, 1) for j in range(4, 9)]
    even = flat[:4] + [flat[4]]
    odd = [jnp.where(low, turned[k], turned[k + 1]) for k in range(4)] + [turned[4]]
    return jnp.concatenate([jnp.concatenate(even, 1), jnp.concatenate(odd, 1)], 0)[:, :ROWS]


def own_store(flat_ref, value, pairs):
    value = jnp.concatenate([value, jnp.zeros((2 * pairs, 64), f32)], 1)
    low = lax.broadcasted_iota(jnp.int32, (pairs, 128), 1) < 64
    even = [value[:pairs, 128 * j : 128 * j + 128] for j in range(5)]
    odd = [pltpu.roll(value[pairs:, 128 * j : 128 * j + 128], 64, 1) for j in range(5)]
    flat = even[:4] + [jnp.where(low, even[4], odd[0])]
    flat += [jnp.where(low, odd[k], odd[k + 1]) for k in range(4)]
    for j in range(9):
        flat_ref[pl.ds(j, pairs, stride=9), :] = flat[j]


def triangle():
    return [(a, min(a + 256, ROWS)) for a in range(0, ROWS, 256)]


def side_by_side(values):
    return jnp.concatenate(values, 1)


def gram_columns(iterate):
    return [lax.dot_general(iterate[a:], iterate[a:b], NT, preferred_element_type=f32) for a, b in triangle()]


def mirror(ref, value, a, b):
    ref[a:, a:b] = value
    if b < ROWS:
        ref[a:b, b:] = value[b - a :].T


def store_poly(columns, low_ref, poly_ref):
    for (a, b), column in zip(triangle(), columns):
        mirror(low_ref, column.astype(bf16), a, b)
    for (a, b), column in zip(triangle(), columns):
        squared = jnp.dot(low_ref[a:, :], low_ref[:, a:b], preferred_element_type=f32)
        mirror(poly_ref, (coef_second * column + coef_third * squared).astype(bf16), a, b)


def gram_kernel(mine_ref, pair_ref, scale_ref, gram_ref, momentum_out_ref):
    iterate = side_by_side([mine_ref[i] for i in range(mine_ref.shape[0])])
    for (a, b), column in zip(triangle(), gram_columns(iterate)):
        gram_ref[a:, a:b] = column
    momentum_out_ref[0] = momentum_rate * pair_ref[1] + scale_ref[0:1, :] * pair_ref[0]


def iterate_kernel(update_scale, mine_ref, other_ref, gram_ref, own_ref, out_ref, poly_ref, next_ref, flat_ref, low_ref):
    blocks = [(r, i) for r in (mine_ref, other_ref) for i in range(r.shape[0])]
    pairs = own_ref.shape[0] // 9
    columns = gram_columns(side_by_side([other_ref[i] for i in range(other_ref.shape[0])]))
    columns = [gram_ref[a:, a:b] + column for (a, b), column in zip(triangle(), columns)]
    store_poly(columns, low_ref, poly_ref)
    for i, (r, k) in enumerate(blocks):
        v = r[k]
        product = jnp.dot(poly_ref[...], v, preferred_element_type=f32)
        next_ref[i] = (coef_first * v.astype(f32) + product).astype(bf16)
    own = own_load(own_ref, pairs)
    product = jnp.dot(own.astype(bf16), poly_ref[...], preferred_element_type=f32)
    own = (coef_first * own + product).astype(bf16)
    store_poly(gram_columns(side_by_side([next_ref[i] for i in range(len(blocks))])), low_ref, poly_ref)
    product = jnp.dot(own, poly_ref[...], preferred_element_type=f32)
    own_store(flat_ref, update_scale * (coef_first * own.astype(f32) + product), pairs)
    out_ref[0] = flat_ref[...].astype(bf16)


def pairings(count, core):
    return [((i + core) % count, (i + core + 1) % count) for i in range(0, count, 2)]


def gather_groups(nx, ny, nc):
    def at(x, y, core):
        return (x * ny + y) * nc + core

    first, second = [], []
    for core in range(nc):
        for xs in pairings(nx, core):
            for parity in range(2):
                first.append([at(x, y, core) for x in xs for y in range(parity, ny, 2)])
        for xs in pairings(nx, 1 - core):
            for ys in pairings(ny, core):
                second.append([at(x, y, core) for x in xs for y in ys])
    return first, second


def kernel(body, name, out, in_specs, scratch=(), cost=None):
    return pl.pallas_call(
        body,
        name=name,
        out_shape=out,
        in_specs=in_specs,
        out_specs=jax.tree.map(lambda _: VMEM, out),
        scratch_shapes=list(scratch),
        compiler_params=pltpu.CompilerParams(vmem_limit_bytes=40 * 2**20),
        cost_estimate=cost,
    )


def local(entries, update_scale, sizes, grad, momentum):
    nx, ny, nc, ng = sizes
    chips = ("x", "y", "core")
    first_groups, second_groups = gather_groups(nx, ny, nc)
    blocks, copies = len(first_groups[0]), len(second_groups[0])
    rows = grad.shape[1]
    columns = blocks * rows * 128 // ROWS
    shape = jax.ShapeDtypeStruct
    group = lax.axis_index("group").astype(jnp.int32).reshape(1)
    grad, momentum, group = lax.optimization_barrier((grad, momentum, group))
    first = lax.broadcasted_iota(jnp.int32, (2, rows, 128), 0) == 0
    pair = jnp.where(first, grad, momentum)
    sums = kernel(sums_kernel, "sums", shape((ny * nc, 128), f32), [VMEM])(pair)
    sums = lax.all_to_all(sums.reshape(-1, 1, 128), ("y", "core"), 0, 0).reshape(-1, 128)
    sums = kernel(functools.partial(combine_kernel, ng), "combine", shape((nx * ng, 128), f32), [SMEM, VMEM])(group, sums)
    sums = lax.all_to_all(sums.reshape(-1, 1, 128), ("x", "group"), 0, 0).reshape(-1, 128)
    iterate, own, scale = kernel(
        functools.partial(scale_kernel, entries),
        "scale",
        (shape((blocks, rows, 128), bf16), shape((rows, 128), f32), shape((8, 128), f32)),
        [VMEM] * 2,
    )(sums, pair)
    gathered = lax.all_to_all(iterate, chips, 0, 0, axis_index_groups=first_groups)
    turned = kernel(
        functools.partial(transpose_kernel, copies),
        "turn",
        shape((copies, ROWS, columns), bf16),
        [VMEM],
        scratch=[pltpu.VMEM((blocks * rows, 128), f32)],
    )(gathered)
    mine = lax.all_to_all(turned, chips, 0, 0, axis_index_groups=second_groups)
    other = lax.ppermute(mine, "core", [(0, 1), (1, 0)])
    gram, momentum_out = kernel(
        gram_kernel,
        "gram",
        (shape((ROWS, ROWS), f32), shape(grad.shape, f32)),
        [VMEM] * 3,
        cost=pl.CostEstimate(flops=2 * ROWS * ROWS * columns * copies, bytes_accessed=2 * ROWS * columns * copies, transcendentals=0),
    )(mine, pair, scale)
    update = kernel(
        functools.partial(iterate_kernel, update_scale),
        "newton",
        shape(grad.shape, bf16),
        [VMEM] * 4,
        scratch=[
            pltpu.VMEM((ROWS, ROWS), bf16),
            pltpu.VMEM((2 * copies, ROWS, columns), bf16),
            pltpu.VMEM((rows, 128), f32),
            pltpu.VMEM((ROWS, ROWS), bf16),
        ],
    )(mine, other, gram, own)
    return momentum_out, update


def solution(mesh):
    sizes = (4, 8, 2, 12)
    split_mesh = Mesh(mesh.devices.reshape(sizes), ("x", "y", "core", "group"))
    spec = P("group", ("x", "y", "core"), None)

    def run(grad, momentum):
        entries = grad.size
        layers, flat_rows, _ = grad.shape
        width = flat_rows * 128 // ROWS
        update_scale = 0.2 * math.sqrt(max(ROWS, width))
        return jax.shard_map(
            functools.partial(local, entries, update_scale, sizes),
            mesh=split_mesh,
            in_specs=(spec, spec),
            out_specs=(spec, spec),
            check_vma=False,
        )(grad, momentum)

    return run
```

```python
import functools
import math

import jax
import jax.numpy as jnp
import numpy as np
from jax import lax
from jax.experimental import pallas as pl
from jax.experimental.pallas import tpu as pltpu
from jax.sharding import Mesh, PartitionSpec as P

ROWS = 576
ITERS = 2

momentum_rate = 0.95
target_rms = 0.5
coef_first = 3.4445
coef_second = -4.775
coef_third = 2.0315

f32, bf16 = jnp.float32, jnp.bfloat16
VMEM = pl.BlockSpec(memory_space=pltpu.VMEM)
SMEM = pl.BlockSpec(memory_space=pltpu.SMEM)
NT = (((1,), (1,)), ((), ()))


def two_sum(a, b):
    s = a + b
    t = s - a
    return s, (a - (s - t)) + (b - t)


def fast_two_sum(a, b):
    s = a + b
    return s, b - (s - a)


def split(a):
    t = 4097.0 * a
    high = t - (t - a)
    return high, a - high


def two_prod(a, b):
    p = a * b
    ah, al = split(a)
    bh, bl = split(b)
    return p, ((ah * bh - p) + ah * bl + al * bh) + al * bl


def dd_add(a, b):
    s, e = two_sum(a[0], b[0])
    return fast_two_sum(s, e + (a[1] + b[1]))


def dd_mul(a, b):
    p, e = two_prod(a[0], b[0])
    return fast_two_sum(p, e + (a[0] * b[1] + a[1] * b[0]))


def dd_const(value):
    high = np.float32(value)
    return float(high), float(np.float32(value - float(high)))


def lazy_add(a, b):
    s, e = two_sum(a[0], b[0])
    return s, (a[1] + b[1]) + e


def tree(values):
    while len(values) > 1:
        paired = [lazy_add(values[i], values[i + 1]) for i in range(0, len(values) - 1, 2)]
        values = paired + ([values[-1]] if len(values) % 2 else [])
    return values[0]


def fold(a, axis, shifts):
    for shift in shifts:
        a = lazy_add(a, (pltpu.roll(a[0], shift, axis), pltpu.roll(a[1], shift, axis)))
    return a


def lanes():
    return lax.broadcasted_iota(jnp.int32, (8, 128), 1)


def pack(values):
    lane = lanes()
    tile = jnp.zeros((8, 128), f32)
    for i, (high, low) in enumerate(values):
        tile = jnp.where(lane == i, high, jnp.where(lane == i + 64, low, tile))
    return tile


def add_rows(ref):
    zero = jnp.zeros((8, 128), f32)
    high, low = fold(tree([(ref[i : i + 8, :], zero) for i in range(0, ref.shape[0], 8)]), 0, (4, 2, 1))
    return fast_two_sum(high, low + pltpu.roll(high, 64, 1))


def sums_kernel(groups, group_ref, pair_ref, out_ref):
    gg, gm, mm = [], [], []
    for i in range(0, pair_ref.shape[1], 8):
        g = pair_ref[0, i : i + 8, :]
        m = pair_ref[1, i : i + 8, :]
        gg.append(two_prod(g, g))
        gm.append(two_prod(g, m))
        mm.append(two_prod(m, m))
    sums = [fold(fold(tree(v), 0, (4, 2, 1)), 1, (64, 32, 16, 8, 4, 2, 1)) for v in (gg, gm, mm)]
    tile = pack([fast_two_sum(*v) for v in [sums[0]] + sums])
    for i in range(0, out_ref.shape[0], 8):
        to = lax.rem(lax.broadcasted_iota(jnp.int32, (8, 128), 0) + i, groups)
        keep = (to == group_ref[0]) | (lax.rem(lanes(), 64) == 0)
        out_ref[i : i + 8, :] = jnp.where(keep, tile, 0.0)


def combine_kernel(in_ref, out_ref):
    high, low = add_rows(in_ref)
    tile = jnp.where(lanes() < 64, high, pltpu.roll(low, 64, 1))
    for i in range(0, out_ref.shape[0], 8):
        out_ref[i : i + 8, :] = tile


def scale_kernel(entries, in_ref, pair_ref, out_ref, own_ref, scale_ref):
    high, low = add_rows(in_ref)
    lane = lanes()

    def value(i):
        return tuple(jnp.sum(jnp.where(lane == i, v, 0.0), axis=1, keepdims=True)[0:1] for v in (high, low))

    square, gg, gm, mm = (value(i) for i in range(4))
    grad_scale = target_rms / (jnp.sqrt(square[0] / entries) + 1e-06)
    rate = float(np.float32(momentum_rate))
    factor_high, factor_low = dd_const(1.0 + rate)
    ones = jnp.ones_like(grad_scale)
    a = two_prod(grad_scale, factor_high * ones)
    a = fast_two_sum(a[0], a[1] + grad_scale * factor_low)
    b = tuple(v * ones for v in dd_const(rate * rate))
    cross = dd_mul(dd_mul((2.0 * a[0], 2.0 * a[1]), b), gm)
    total = dd_add(dd_add(dd_mul(a, dd_mul(a, gg)), dd_mul(dd_mul(b, b), mm)), cross)
    unorm = jnp.sqrt(jnp.maximum(total[0], 0.0))
    scaled_grad = grad_scale * pair_ref[0]
    nudged = scaled_grad + momentum_rate * (momentum_rate * pair_ref[1] + scaled_grad)
    iterate = (nudged / (unorm + 1e-07)).astype(bf16)
    for i in range(out_ref.shape[0]):
        out_ref[i] = iterate
    own_ref[...] = iterate.astype(f32)
    scale_ref[...] = jnp.broadcast_to(grad_scale, scale_ref.shape)


def transpose_kernel(copies, in_ref, out_ref, flat_ref):
    blocks, rows = in_ref.shape[:2]
    for i in range(blocks):
        flat_ref[i * rows : (i + 1) * rows, :] = in_ref[i].astype(f32)
    half = blocks * rows // 9
    for j in range(9):
        turned = flat_ref[pl.ds(j, half, stride=9), :].T.astype(bf16)
        for i in range(copies):
            if j < 4:
                out_ref[i, 128 * j : 128 * j + 128, 0:half] = turned
            elif j == 4:
                out_ref[i, 512:576, 0:half] = turned[0:64]
                out_ref[i, 0:64, half : 2 * half] = turned[64:128]
            else:
                out_ref[i, 128 * j - 576 : 128 * j - 448, half : 2 * half] = turned


def own_load(flat_ref, pairs):
    low = lax.broadcasted_iota(jnp.int32, (pairs, 128), 1) < 64
    flat = [flat_ref[pl.ds(j, pairs, stride=9), :] for j in range(9)]
    turned = [pltpu.roll(flat[j], 64, 1) for j in range(4, 9)]
    even = flat[:4] + [flat[4]]
    odd = [jnp.where(low, turned[k], turned[k + 1]) for k in range(4)] + [turned[4]]
    return jnp.concatenate([jnp.concatenate(even, 1), jnp.concatenate(odd, 1)], 0)[:, :ROWS]


def own_store(flat_ref, value, pairs):
    value = jnp.concatenate([value, jnp.zeros((2 * pairs, 64), f32)], 1)
    low = lax.broadcasted_iota(jnp.int32, (pairs, 128), 1) < 64
    even = [value[:pairs, 128 * j : 128 * j + 128] for j in range(5)]
    odd = [pltpu.roll(value[pairs:, 128 * j : 128 * j + 128], 64, 1) for j in range(5)]
    flat = even[:4] + [jnp.where(low, even[4], odd[0])]
    flat += [jnp.where(low, odd[k], odd[k + 1]) for k in range(4)]
    for j in range(9):
        flat_ref[pl.ds(j, pairs, stride=9), :] = flat[j]


def triangle():
    return [(a, min(a + 256, ROWS)) for a in range(0, ROWS, 256)]


def side_by_side(values):
    return jnp.concatenate(values, 1)


def gram_columns(iterate):
    return [lax.dot_general(iterate[a:], iterate[a:b], NT, preferred_element_type=f32) for a, b in triangle()]


def mirror(ref, value, a, b):
    ref[a:, a:b] = value
    if b < ROWS:
        ref[a:b, b:] = value[b - a :].T


def store_poly(columns, low_ref, poly_ref):
    for (a, b), column in zip(triangle(), columns):
        mirror(low_ref, column.astype(bf16), a, b)
    for (a, b), column in zip(triangle(), columns):
        squared = jnp.dot(low_ref[a:, :], low_ref[:, a:b], preferred_element_type=f32)
        mirror(poly_ref, (coef_second * column + coef_third * squared).astype(bf16), a, b)


def gram_kernel(mine_ref, pair_ref, scale_ref, gram_ref, momentum_out_ref):
    iterate = side_by_side([mine_ref[i] for i in range(mine_ref.shape[0])])
    for (a, b), column in zip(triangle(), gram_columns(iterate)):
        gram_ref[a:, a:b] = column
    momentum_out_ref[0] = momentum_rate * pair_ref[1] + scale_ref[0:1, :] * pair_ref[0]


def iterate_kernel(update_scale, mine_ref, other_ref, gram_ref, own_ref, out_ref, poly_ref, next_ref, flat_ref, low_ref):
    blocks = [(r, i) for r in (mine_ref, other_ref) for i in range(r.shape[0])]
    pairs = own_ref.shape[0] // 9
    columns = gram_columns(side_by_side([other_ref[i] for i in range(other_ref.shape[0])]))
    columns = [gram_ref[a:, a:b] + column for (a, b), column in zip(triangle(), columns)]
    store_poly(columns, low_ref, poly_ref)
    for i, (r, k) in enumerate(blocks):
        v = r[k]
        product = jnp.dot(poly_ref[...], v, preferred_element_type=f32)
        next_ref[i] = (coef_first * v.astype(f32) + product).astype(bf16)
    own = own_load(own_ref, pairs)
    product = jnp.dot(own.astype(bf16), poly_ref[...], preferred_element_type=f32)
    own = (coef_first * own + product).astype(bf16)
    store_poly(gram_columns(side_by_side([next_ref[i] for i in range(len(blocks))])), low_ref, poly_ref)
    product = jnp.dot(own, poly_ref[...], preferred_element_type=f32)
    own_store(flat_ref, update_scale * (coef_first * own.astype(f32) + product), pairs)
    out_ref[0] = flat_ref[...].astype(bf16)


def pairings(count, core):
    return [((i + core) % count, (i + core + 1) % count) for i in range(0, count, 2)]


def gather_groups(nx, ny, nc):
    def at(x, y, core):
        return (x * ny + y) * nc + core

    first, second = [], []
    for core in range(nc):
        for xs in pairings(nx, core):
            for parity in range(2):
                first.append([at(x, y, core) for x in xs for y in range(parity, ny, 2)])
        for xs in pairings(nx, 1 - core):
            for ys in pairings(ny, core):
                second.append([at(x, y, core) for x in xs for y in ys])
    return first, second


def kernel(body, name, out, in_specs, scratch=(), cost=None):
    return pl.pallas_call(
        body,
        name=name,
        out_shape=out,
        in_specs=in_specs,
        out_specs=jax.tree.map(lambda _: VMEM, out),
        scratch_shapes=list(scratch),
        compiler_params=pltpu.CompilerParams(vmem_limit_bytes=40 * 2**20),
        cost_estimate=cost,
    )


def local(entries, update_scale, sizes, grad, momentum):
    nx, ny, nc, ng = sizes
    chips = ("x", "y", "core")
    first_groups, second_groups = gather_groups(nx, ny, nc)
    blocks, copies = len(first_groups[0]), len(second_groups[0])
    rows = grad.shape[1]
    columns = blocks * rows * 128 // ROWS
    shape = jax.ShapeDtypeStruct
    group = lax.axis_index("group").astype(jnp.int32).reshape(1)
    grad, momentum, group = lax.optimization_barrier((grad, momentum, group))
    first = lax.broadcasted_iota(jnp.int32, (2, rows, 128), 0) == 0
    pair = jnp.where(first, grad, momentum)
    sums = kernel(functools.partial(sums_kernel, ng), "sums", shape((nx * ng, 128), f32), [SMEM, VMEM])(group, pair)
    sums = lax.all_to_all(sums.reshape(-1, 1, 128), ("x", "group"), 0, 0).reshape(-1, 128)
    sums = kernel(combine_kernel, "combine", shape((ny * nc, 128), f32), [VMEM])(sums)
    sums = lax.all_to_all(sums.reshape(-1, 1, 128), ("y", "core"), 0, 0).reshape(-1, 128)
    iterate, own, scale = kernel(
        functools.partial(scale_kernel, entries),
        "scale",
        (shape((blocks, rows, 128), bf16), shape((rows, 128), f32), shape((8, 128), f32)),
        [VMEM] * 2,
    )(sums, pair)
    gathered = lax.all_to_all(iterate, chips, 0, 0, axis_index_groups=first_groups)
    turned = kernel(
        functools.partial(transpose_kernel, copies),
        "turn",
        shape((copies, ROWS, columns), bf16),
        [VMEM],
        scratch=[pltpu.VMEM((blocks * rows, 128), f32)],
    )(gathered)
    mine = lax.all_to_all(turned, chips, 0, 0, axis_index_groups=second_groups)
    other = lax.ppermute(mine, "core", [(0, 1), (1, 0)])
    gram, momentum_out = kernel(
        gram_kernel,
        "gram",
        (shape((ROWS, ROWS), f32), shape(grad.shape, f32)),
        [VMEM] * 3,
        cost=pl.CostEstimate(flops=2 * ROWS * ROWS * columns * copies, bytes_accessed=2 * ROWS * columns * copies, transcendentals=0),
    )(mine, pair, scale)
    update = kernel(
        functools.partial(iterate_kernel, update_scale),
        "newton",
        shape(grad.shape, bf16),
        [VMEM] * 4,
        scratch=[
            pltpu.VMEM((ROWS, ROWS), bf16),
            pltpu.VMEM((2 * copies, ROWS, columns), bf16),
            pltpu.VMEM((rows, 128), f32),
            pltpu.VMEM((ROWS, ROWS), bf16),
        ],
    )(mine, other, gram, own)
    return momentum_out, update


def solution(mesh):
    sizes = (4, 8, 2, 12)
    split_mesh = Mesh(mesh.devices.reshape(sizes), ("x", "y", "core", "group"))
    spec = P("group", ("x", "y", "core"), None)

    def run(grad, momentum):
        entries = grad.size
        layers, flat_rows, _ = grad.shape
        width = flat_rows * 128 // ROWS
        update_scale = 0.2 * math.sqrt(max(ROWS, width))
        return jax.shard_map(
            functools.partial(local, entries, update_scale, sizes),
            mesh=split_mesh,
            in_specs=(spec, spec),
            out_specs=(spec, spec),
            check_vma=False,
        )(grad, momentum)

    return run
```

```python
import functools
import math

import jax
import jax.numpy as jnp
import numpy as np
from jax import lax
from jax.experimental import pallas as pl
from jax.experimental.pallas import tpu as pltpu
from jax.sharding import Mesh, PartitionSpec as P

ROWS = 576
ITERS = 2

momentum_rate = 0.95
target_rms = 0.5
coef_first = 3.4445
coef_second = -4.775
coef_third = 2.0315

f32, bf16 = jnp.float32, jnp.bfloat16
VMEM = pl.BlockSpec(memory_space=pltpu.VMEM)
SMEM = pl.BlockSpec(memory_space=pltpu.SMEM)
NT = (((1,), (1,)), ((), ()))


def two_sum(a, b):
    s = a + b
    t = s - a
    return s, (a - (s - t)) + (b - t)


def fast_two_sum(a, b):
    s = a + b
    return s, b - (s - a)


def split(a):
    t = 4097.0 * a
    high = t - (t - a)
    return high, a - high


def two_prod(a, b):
    p = a * b
    ah, al = split(a)
    bh, bl = split(b)
    return p, ((ah * bh - p) + ah * bl + al * bh) + al * bl


def dd_add(a, b):
    s, e = two_sum(a[0], b[0])
    return fast_two_sum(s, e + (a[1] + b[1]))


def dd_mul(a, b):
    p, e = two_prod(a[0], b[0])
    return fast_two_sum(p, e + (a[0] * b[1] + a[1] * b[0]))


def dd_const(value):
    high = np.float32(value)
    return float(high), float(np.float32(value - float(high)))


def lazy_add(a, b):
    s, e = two_sum(a[0], b[0])
    return s, (a[1] + b[1]) + e


def tree(values):
    while len(values) > 1:
        paired = [lazy_add(values[i], values[i + 1]) for i in range(0, len(values) - 1, 2)]
        values = paired + ([values[-1]] if len(values) % 2 else [])
    return values[0]


def fold(a, axis, shifts):
    for shift in shifts:
        a = lazy_add(a, (pltpu.roll(a[0], shift, axis), pltpu.roll(a[1], shift, axis)))
    return a


def lanes():
    return lax.broadcasted_iota(jnp.int32, (8, 128), 1)


def pack(values):
    lane = lanes()
    tile = jnp.zeros((8, 128), f32)
    for i, (high, low) in enumerate(values):
        tile = jnp.where(lane == i, high, jnp.where(lane == i + 64, low, tile))
    return tile


def add_rows(ref):
    zero = jnp.zeros((8, 128), f32)
    high, low = fold(tree([(ref[i : i + 8, :], zero) for i in range(0, ref.shape[0], 8)]), 0, (4, 2, 1))
    return fast_two_sum(high, low + pltpu.roll(high, 64, 1))


def sums_kernel(pair_ref, out_ref):
    gg, gm, mm = [], [], []
    for i in range(0, pair_ref.shape[1], 8):
        g = pair_ref[0, i : i + 8, :]
        m = pair_ref[1, i : i + 8, :]
        gg.append(two_prod(g, g))
        gm.append(two_prod(g, m))
        mm.append(two_prod(m, m))
    sums = [fold(fold(tree(v), 0, (4, 2, 1)), 1, (64, 32, 16, 8, 4, 2, 1)) for v in (gg, gm, mm)]
    tile = pack([fast_two_sum(*v) for v in [sums[0]] + sums])
    for i in range(0, out_ref.shape[0], 8):
        out_ref[i : i + 8, :] = tile


def combine_kernel(groups, group_ref, in_ref, out_ref):
    high, low = add_rows(in_ref)
    lane = lanes()
    tile = jnp.where(lane < 64, high, pltpu.roll(low, 64, 1))
    for i in range(0, out_ref.shape[0], 8):
        to = lax.rem(lax.broadcasted_iota(jnp.int32, (8, 128), 0) + i, groups)
        keep = (to == group_ref[0]) | (lax.rem(lane, 64) == 0)
        out_ref[i : i + 8, :] = jnp.where(keep, tile, 0.0)


def scale_kernel(entries, in_ref, pair_ref, out_ref, own_ref, scale_ref):
    high, low = add_rows(in_ref)
    lane = lanes()

    def value(i):
        return tuple(jnp.sum(jnp.where(lane == i, v, 0.0), axis=1, keepdims=True)[0:1] for v in (high, low))

    square, gg, gm, mm = (value(i) for i in range(4))
    grad_scale = target_rms / (jnp.sqrt(square[0] / entries) + 1e-06)
    rate = float(np.float32(momentum_rate))
    factor_high, factor_low = dd_const(1.0 + rate)
    ones = jnp.ones_like(grad_scale)
    a = two_prod(grad_scale, factor_high * ones)
    a = fast_two_sum(a[0], a[1] + grad_scale * factor_low)
    b = tuple(v * ones for v in dd_const(rate * rate))
    cross = dd_mul(dd_mul((2.0 * a[0], 2.0 * a[1]), b), gm)
    total = dd_add(dd_add(dd_mul(a, dd_mul(a, gg)), dd_mul(dd_mul(b, b), mm)), cross)
    unorm = jnp.sqrt(jnp.maximum(total[0], 0.0))
    scaled_grad = grad_scale * pair_ref[0]
    nudged = scaled_grad + momentum_rate * (momentum_rate * pair_ref[1] + scaled_grad)
    iterate = (nudged / (unorm + 1e-07)).astype(bf16)
    for i in range(out_ref.shape[0]):
        out_ref[i] = iterate
    own_ref[...] = iterate.astype(f32)
    scale_ref[...] = jnp.broadcast_to(grad_scale, scale_ref.shape)


def transpose_kernel(copies, in_ref, out_ref, flat_ref):
    blocks, rows = in_ref.shape[:2]
    for i in range(blocks):
        flat_ref[i * rows : (i + 1) * rows, :] = in_ref[i].astype(f32)
    half = blocks * rows // 9
    for j in range(9):
        turned = flat_ref[pl.ds(j, half, stride=9), :].T.astype(bf16)
        for i in range(copies):
            if j < 4:
                out_ref[i, 128 * j : 128 * j + 128, 0:half] = turned
            elif j == 4:
                out_ref[i, 512:576, 0:half] = turned[0:64]
                out_ref[i, 0:64, half : 2 * half] = turned[64:128]
            else:
                out_ref[i, 128 * j - 576 : 128 * j - 448, half : 2 * half] = turned


def own_load(flat_ref, pairs):
    low = lax.broadcasted_iota(jnp.int32, (pairs, 128), 1) < 64
    flat = [flat_ref[pl.ds(j, pairs, stride=9), :] for j in range(9)]
    turned = [pltpu.roll(flat[j], 64, 1) for j in range(4, 9)]
    even = flat[:4] + [flat[4]]
    odd = [jnp.where(low, turned[k], turned[k + 1]) for k in range(4)] + [turned[4]]
    return jnp.concatenate([jnp.concatenate(even, 1), jnp.concatenate(odd, 1)], 0)[:, :ROWS]


def own_store(flat_ref, value, pairs):
    value = jnp.concatenate([value, jnp.zeros((2 * pairs, 64), f32)], 1)
    low = lax.broadcasted_iota(jnp.int32, (pairs, 128), 1) < 64
    even = [value[:pairs, 128 * j : 128 * j + 128] for j in range(5)]
    odd = [pltpu.roll(value[pairs:, 128 * j : 128 * j + 128], 64, 1) for j in range(5)]
    flat = even[:4] + [jnp.where(low, even[4], odd[0])]
    flat += [jnp.where(low, odd[k], odd[k + 1]) for k in range(4)]
    for j in range(9):
        flat_ref[pl.ds(j, pairs, stride=9), :] = flat[j]


def triangle():
    return [(a, min(a + 256, ROWS)) for a in range(0, ROWS, 256)]


def side_by_side(values):
    return jnp.concatenate(values, 1)


def gram_columns(iterate):
    return [lax.dot_general(iterate[a:], iterate[a:b], NT, preferred_element_type=f32) for a, b in triangle()]


def mirror(ref, value, a, b):
    ref[a:, a:b] = value
    if b < ROWS:
        ref[a:b, b:] = value[b - a :].T


def store_poly(columns, low_ref, poly_ref):
    for (a, b), column in zip(triangle(), columns):
        mirror(low_ref, column.astype(bf16), a, b)
    for (a, b), column in zip(triangle(), columns):
        squared = jnp.dot(low_ref[a:, :], low_ref[:, a:b], preferred_element_type=f32)
        mirror(poly_ref, (coef_second * column + coef_third * squared).astype(bf16), a, b)


def gram_kernel(mine_ref, pair_ref, scale_ref, gram_ref, momentum_out_ref):
    iterate = side_by_side([mine_ref[i] for i in range(mine_ref.shape[0])])
    for (a, b), column in zip(triangle(), gram_columns(iterate)):
        gram_ref[a:, a:b] = column
    momentum_out_ref[0] = momentum_rate * pair_ref[1] + scale_ref[0:1, :] * pair_ref[0]


def iterate_kernel(update_scale, mine_ref, other_ref, gram_ref, own_ref, out_ref, poly_ref, next_ref, flat_ref, low_ref):
    blocks = [(r, i) for r in (mine_ref, other_ref) for i in range(r.shape[0])]
    pairs = own_ref.shape[0] // 9
    columns = gram_columns(side_by_side([other_ref[i] for i in range(other_ref.shape[0])]))
    columns = [gram_ref[a:, a:b] + column for (a, b), column in zip(triangle(), columns)]
    store_poly(columns, low_ref, poly_ref)
    for i, (r, k) in enumerate(blocks):
        v = r[k]
        product = jnp.dot(poly_ref[...], v, preferred_element_type=f32)
        next_ref[i] = (coef_first * v.astype(f32) + product).astype(bf16)
    columns = gram_columns(side_by_side([next_ref[i] for i in range(len(blocks))]))
    own = own_load(own_ref, pairs)
    product = jnp.dot(own.astype(bf16), poly_ref[...], preferred_element_type=f32)
    own = (coef_first * own + product).astype(bf16)
    store_poly(columns, low_ref, poly_ref)
    product = side_by_side([jnp.dot(own, poly_ref[:, a:b], preferred_element_type=f32) for a, b in triangle()])
    own_store(flat_ref, update_scale * (coef_first * own.astype(f32) + product), pairs)
    out_ref[0] = flat_ref[...].astype(bf16)


def pairings(count, core):
    return [((i + core) % count, (i + core + 1) % count) for i in range(0, count, 2)]


def gather_groups(nx, ny, nc):
    def at(x, y, core):
        return (x * ny + y) * nc + core

    first, second = [], []
    for core in range(nc):
        for xs in pairings(nx, core):
            for parity in range(2):
                first.append([at(x, y, core) for x in xs for y in range(parity, ny, 2)])
        for xs in pairings(nx, 1 - core):
            for ys in pairings(ny, core):
                second.append([at(x, y, core) for x in xs for y in ys])
    return first, second


def kernel(body, name, out, in_specs, scratch=(), cost=None):
    return pl.pallas_call(
        body,
        name=name,
        out_shape=out,
        in_specs=in_specs,
        out_specs=jax.tree.map(lambda _: VMEM, out),
        scratch_shapes=list(scratch),
        compiler_params=pltpu.CompilerParams(vmem_limit_bytes=40 * 2**20),
        cost_estimate=cost,
    )


def local(entries, update_scale, sizes, grad, momentum):
    nx, ny, nc, ng = sizes
    chips = ("x", "y", "core")
    first_groups, second_groups = gather_groups(nx, ny, nc)
    blocks, copies = len(first_groups[0]), len(second_groups[0])
    rows = grad.shape[1]
    columns = blocks * rows * 128 // ROWS
    shape = jax.ShapeDtypeStruct
    group = lax.axis_index("group").astype(jnp.int32).reshape(1)
    grad, momentum, group = lax.optimization_barrier((grad, momentum, group))
    first = lax.broadcasted_iota(jnp.int32, (2, rows, 128), 0) == 0
    pair = jnp.where(first, grad, momentum)
    sums = kernel(sums_kernel, "sums", shape((ny * nc, 128), f32), [VMEM])(pair)
    sums = lax.all_to_all(sums.reshape(-1, 1, 128), ("y", "core"), 0, 0).reshape(-1, 128)
    sums = kernel(functools.partial(combine_kernel, ng), "combine", shape((nx * ng, 128), f32), [SMEM, VMEM])(group, sums)
    sums = lax.all_to_all(sums.reshape(-1, 1, 128), ("x", "group"), 0, 0).reshape(-1, 128)
    iterate, own, scale = kernel(
        functools.partial(scale_kernel, entries),
        "scale",
        (shape((blocks, rows, 128), bf16), shape((rows, 128), f32), shape((8, 128), f32)),
        [VMEM] * 2,
    )(sums, pair)
    gathered = lax.all_to_all(iterate, chips, 0, 0, axis_index_groups=first_groups)
    turned = kernel(
        functools.partial(transpose_kernel, copies),
        "turn",
        shape((copies, ROWS, columns), bf16),
        [VMEM],
        scratch=[pltpu.VMEM((blocks * rows, 128), f32)],
    )(gathered)
    mine = lax.all_to_all(turned, chips, 0, 0, axis_index_groups=second_groups)
    other = lax.ppermute(mine, "core", [(0, 1), (1, 0)])
    gram, momentum_out = kernel(
        gram_kernel,
        "gram",
        (shape((ROWS, ROWS), f32), shape(grad.shape, f32)),
        [VMEM] * 3,
        cost=pl.CostEstimate(flops=2 * ROWS * ROWS * columns * copies, bytes_accessed=2 * ROWS * columns * copies, transcendentals=0),
    )(mine, pair, scale)
    update = kernel(
        functools.partial(iterate_kernel, update_scale),
        "newton",
        shape(grad.shape, bf16),
        [VMEM] * 4,
        scratch=[
            pltpu.VMEM((ROWS, ROWS), bf16),
            pltpu.VMEM((2 * copies, ROWS, columns), bf16),
            pltpu.VMEM((rows, 128), f32),
            pltpu.VMEM((ROWS, ROWS), bf16),
        ],
    )(mine, other, gram, own)
    return momentum_out, update


def solution(mesh):
    sizes = (4, 8, 2, 12)
    split_mesh = Mesh(mesh.devices.reshape(sizes), ("x", "y", "core", "group"))
    spec = P("group", ("x", "y", "core"), None)

    def run(grad, momentum):
        entries = grad.size
        layers, flat_rows, _ = grad.shape
        width = flat_rows * 128 // ROWS
        update_scale = 0.2 * math.sqrt(max(ROWS, width))
        return jax.shard_map(
            functools.partial(local, entries, update_scale, sizes),
            mesh=split_mesh,
            in_specs=(spec, spec),
            out_specs=(spec, spec),
            check_vma=False,
        )(grad, momentum)

    return run
```

```python
import functools
import math

import jax
import jax.numpy as jnp
import numpy as np
from jax import lax
from jax.experimental import pallas as pl
from jax.experimental.pallas import tpu as pltpu
from jax.sharding import Mesh, PartitionSpec as P

ROWS = 576
ITERS = 2

momentum_rate = 0.95
target_rms = 0.5
coef_first = 3.4445
coef_second = -4.775
coef_third = 2.0315

f32, bf16 = jnp.float32, jnp.bfloat16
VMEM = pl.BlockSpec(memory_space=pltpu.VMEM)
SMEM = pl.BlockSpec(memory_space=pltpu.SMEM)
NT = (((1,), (1,)), ((), ()))


def two_sum(a, b):
    s = a + b
    t = s - a
    return s, (a - (s - t)) + (b - t)


def fast_two_sum(a, b):
    s = a + b
    return s, b - (s - a)


def split(a):
    t = 4097.0 * a
    high = t - (t - a)
    return high, a - high


def two_prod(a, b):
    p = a * b
    ah, al = split(a)
    bh, bl = split(b)
    return p, ((ah * bh - p) + ah * bl + al * bh) + al * bl


def dd_add(a, b):
    s, e = two_sum(a[0], b[0])
    return fast_two_sum(s, e + (a[1] + b[1]))


def dd_mul(a, b):
    p, e = two_prod(a[0], b[0])
    return fast_two_sum(p, e + (a[0] * b[1] + a[1] * b[0]))


def dd_const(value):
    high = np.float32(value)
    return float(high), float(np.float32(value - float(high)))


def lazy_add(a, b):
    s, e = two_sum(a[0], b[0])
    return s, (a[1] + b[1]) + e


def tree(values):
    while len(values) > 1:
        paired = [lazy_add(values[i], values[i + 1]) for i in range(0, len(values) - 1, 2)]
        values = paired + ([values[-1]] if len(values) % 2 else [])
    return values[0]


def fold(a, axis, shifts):
    for shift in shifts:
        a = lazy_add(a, (pltpu.roll(a[0], shift, axis), pltpu.roll(a[1], shift, axis)))
    return a


def lanes():
    return lax.broadcasted_iota(jnp.int32, (8, 128), 1)


def pack(values):
    lane = lanes()
    tile = jnp.zeros((8, 128), f32)
    for i, (high, low) in enumerate(values):
        tile = jnp.where(lane == i, high, jnp.where(lane == i + 64, low, tile))
    return tile


def add_rows(ref):
    zero = jnp.zeros((8, 128), f32)
    high, low = fold(tree([(ref[i : i + 8, :], zero) for i in range(0, ref.shape[0], 8)]), 0, (4, 2, 1))
    return fast_two_sum(high, low + pltpu.roll(high, 64, 1))


def sums_kernel(pair_ref, out_ref):
    gg, gm, mm = [], [], []
    for i in range(0, pair_ref.shape[1], 8):
        g = pair_ref[0, i : i + 8, :]
        m = pair_ref[1, i : i + 8, :]
        gg.append(two_prod(g, g))
        gm.append(two_prod(g, m))
        mm.append(two_prod(m, m))
    sums = [fold(fold(tree(v), 0, (4, 2, 1)), 1, (64, 32, 16, 8, 4, 2, 1)) for v in (gg, gm, mm)]
    tile = pack([fast_two_sum(*v) for v in [sums[0]] + sums])
    for i in range(0, out_ref.shape[0], 8):
        out_ref[i : i + 8, :] = tile


def combine_kernel(groups, group_ref, in_ref, out_ref):
    high, low = add_rows(in_ref)
    lane = lanes()
    tile = jnp.where(lane < 64, high, pltpu.roll(low, 64, 1))
    for i in range(0, out_ref.shape[0], 8):
        to = lax.rem(lax.broadcasted_iota(jnp.int32, (8, 128), 0) + i, groups)
        keep = (to == group_ref[0]) | (lax.rem(lane, 64) == 0)
        out_ref[i : i + 8, :] = jnp.where(keep, tile, 0.0)


def scale_kernel(entries, in_ref, pair_ref, out_ref, own_ref, scale_ref):
    high, low = add_rows(in_ref)
    lane = lanes()

    def value(i):
        return tuple(jnp.sum(jnp.where(lane == i, v, 0.0), axis=1, keepdims=True)[0:1] for v in (high, low))

    square, gg, gm, mm = (value(i) for i in range(4))
    grad_scale = target_rms / (jnp.sqrt(square[0] / entries) + 1e-06)
    rate = float(np.float32(momentum_rate))
    factor_high, factor_low = dd_const(1.0 + rate)
    ones = jnp.ones_like(grad_scale)
    a = two_prod(grad_scale, factor_high * ones)
    a = fast_two_sum(a[0], a[1] + grad_scale * factor_low)
    b = tuple(v * ones for v in dd_const(rate * rate))
    cross = dd_mul(dd_mul((2.0 * a[0], 2.0 * a[1]), b), gm)
    total = dd_add(dd_add(dd_mul(a, dd_mul(a, gg)), dd_mul(dd_mul(b, b), mm)), cross)
    unorm = jnp.sqrt(jnp.maximum(total[0], 0.0))
    scaled_grad = grad_scale * pair_ref[0]
    nudged = scaled_grad + momentum_rate * (momentum_rate * pair_ref[1] + scaled_grad)
    iterate = (nudged / (unorm + 1e-07)).astype(bf16)
    for i in range(out_ref.shape[0]):
        out_ref[i] = iterate
    own_ref[...] = iterate.astype(f32)
    scale_ref[...] = jnp.broadcast_to(grad_scale, scale_ref.shape)


def transpose_kernel(copies, in_ref, out_ref, flat_ref):
    blocks, rows = in_ref.shape[:2]
    for i in range(blocks):
        flat_ref[i * rows : (i + 1) * rows, :] = in_ref[i].astype(f32)
    half = blocks * rows // 9
    for j in range(9):
        turned = flat_ref[pl.ds(j, half, stride=9), :].T.astype(bf16)
        for i in range(copies):
            if j < 4:
                out_ref[i, 128 * j : 128 * j + 128, 0:half] = turned
            elif j == 4:
                out_ref[i, 512:576, 0:half] = turned[0:64]
                out_ref[i, 0:64, half : 2 * half] = turned[64:128]
            else:
                out_ref[i, 128 * j - 576 : 128 * j - 448, half : 2 * half] = turned


def own_load(flat_ref, pairs):
    low = lax.broadcasted_iota(jnp.int32, (pairs, 128), 1) < 64
    flat = [flat_ref[pl.ds(j, pairs, stride=9), :] for j in range(9)]
    turned = [pltpu.roll(flat[j], 64, 1) for j in range(4, 9)]
    even = flat[:4] + [flat[4]]
    odd = [jnp.where(low, turned[k], turned[k + 1]) for k in range(4)] + [turned[4]]
    return jnp.concatenate([jnp.concatenate(even, 1), jnp.concatenate(odd, 1)], 0)[:, :ROWS]


def own_store(flat_ref, value, pairs):
    value = jnp.concatenate([value, jnp.zeros((2 * pairs, 64), f32)], 1)
    low = lax.broadcasted_iota(jnp.int32, (pairs, 128), 1) < 64
    even = [value[:pairs, 128 * j : 128 * j + 128] for j in range(5)]
    odd = [pltpu.roll(value[pairs:, 128 * j : 128 * j + 128], 64, 1) for j in range(5)]
    flat = even[:4] + [jnp.where(low, even[4], odd[0])]
    flat += [jnp.where(low, odd[k], odd[k + 1]) for k in range(4)]
    for j in range(9):
        flat_ref[pl.ds(j, pairs, stride=9), :] = flat[j]


def triangle():
    return [(a, min(a + 256, ROWS)) for a in range(0, ROWS, 256)]


def side_by_side(values):
    return jnp.concatenate(values, 1)


def gram_columns(iterate):
    return [lax.dot_general(iterate[a:], iterate[a:b], NT, preferred_element_type=f32) for a, b in triangle()]


def mirror(ref, value, a, b):
    ref[a:, a:b] = value
    if b < ROWS:
        ref[a:b, b:] = value[b - a :].T


def store_poly(columns, low_ref, poly_ref):
    for (a, b), column in zip(triangle(), columns):
        mirror(low_ref, column.astype(bf16), a, b)
    for (a, b), column in zip(triangle(), columns):
        squared = jnp.dot(low_ref[a:, :], low_ref[:, a:b], preferred_element_type=f32)
        mirror(poly_ref, (coef_second * column + coef_third * squared).astype(bf16), a, b)


def joined(ref):
    return side_by_side([ref[i] for i in range(ref.shape[0])])


def gram_kernel(block_ref, pair_ref, scale_ref, gram_ref, momentum_out_ref):
    for (a, b), column in zip(triangle(), gram_columns(joined(block_ref))):
        gram_ref[a:, a:b] = column
    momentum_out_ref[0] = momentum_rate * pair_ref[1] + scale_ref[0:1, :] * pair_ref[0]


def more_gram_kernel(block_ref, gram_ref, out_ref):
    for (a, b), column in zip(triangle(), gram_columns(joined(block_ref))):
        out_ref[a:, a:b] = gram_ref[a:, a:b] + column


def iterate_kernel(update_scale, parts, *refs):
    block_refs = refs[:parts]
    gram_ref, own_ref, out_ref, poly_ref, next_ref, flat_ref, low_ref = refs[parts:]
    blocks = [side_by_side([r[i], r[i + 1]]) for r in block_refs for i in range(0, r.shape[0], 2)]
    pairs = own_ref.shape[0] // 9
    columns = gram_columns(joined(block_refs[-1]))
    columns = [gram_ref[a:, a:b] + column for (a, b), column in zip(triangle(), columns)]
    store_poly(columns, low_ref, poly_ref)
    for i, v in enumerate(blocks):
        product = jnp.dot(poly_ref[...], v, preferred_element_type=f32)
        next_ref[i] = (coef_first * v.astype(f32) + product).astype(bf16)
    columns = gram_columns(joined(next_ref))
    own = own_load(own_ref, pairs)
    product = jnp.dot(own.astype(bf16), poly_ref[...], preferred_element_type=f32)
    own = (coef_first * own + product).astype(bf16)
    store_poly(columns, low_ref, poly_ref)
    product = side_by_side([jnp.dot(own, poly_ref[:, a:b], preferred_element_type=f32) for a, b in triangle()])
    own_store(flat_ref, update_scale * (coef_first * own.astype(f32) + product), pairs)
    out_ref[0] = flat_ref[...].astype(bf16)


def pairings(count, core):
    return [((i + core) % count, (i + core + 1) % count) for i in range(0, count, 2)]


def gather_groups(nx, ny, nc):
    def at(x, y, core):
        return (x * ny + y) * nc + core

    first, second, swap, cores = [], [], [], []
    for core in range(nc):
        for x in range(nx):
            first += [[at(x, y, core) for y in range(parity, ny, 2)] for parity in range(2)]
            cores += [(at(x, y, core), at(x, y, 1 - core)) for y in range(ny)]
        for xs in pairings(nx, core):
            second += [[at(x, y, core) for x in xs for y in ys] for ys in pairings(ny, core)]
        for x, other in pairings(nx, 1 - core):
            for y in range(ny):
                swap += [(at(x, y, core), at(other, y, core)), (at(other, y, core), at(x, y, core))]
    return first, second, swap, cores


def kernel(body, name, out, in_specs, scratch=(), cost=None):
    return pl.pallas_call(
        body,
        name=name,
        out_shape=out,
        in_specs=in_specs,
        out_specs=jax.tree.map(lambda _: VMEM, out),
        scratch_shapes=list(scratch),
        compiler_params=pltpu.CompilerParams(vmem_limit_bytes=40 * 2**20),
        cost_estimate=cost,
    )


def local(entries, update_scale, sizes, grad, momentum):
    nx, ny, nc, ng = sizes
    chips = ("x", "y", "core")
    first_groups, second_groups, swap, cores = gather_groups(nx, ny, nc)
    blocks, copies = len(first_groups[0]), len(second_groups[0])
    rows = grad.shape[1]
    columns = blocks * rows * 128 // ROWS
    shape = jax.ShapeDtypeStruct
    group = lax.axis_index("group").astype(jnp.int32).reshape(1)
    grad, momentum, group = lax.optimization_barrier((grad, momentum, group))
    first = lax.broadcasted_iota(jnp.int32, (2, rows, 128), 0) == 0
    pair = jnp.where(first, grad, momentum)
    sums = kernel(sums_kernel, "sums", shape((ny * nc, 128), f32), [VMEM])(pair)
    sums = lax.all_to_all(sums.reshape(-1, 1, 128), ("y", "core"), 0, 0).reshape(-1, 128)
    sums = kernel(functools.partial(combine_kernel, ng), "combine", shape((nx * ng, 128), f32), [SMEM, VMEM])(group, sums)
    sums = lax.all_to_all(sums.reshape(-1, 1, 128), ("x", "group"), 0, 0).reshape(-1, 128)
    iterate, own, scale = kernel(
        functools.partial(scale_kernel, entries),
        "scale",
        (shape((blocks, rows, 128), bf16), shape((rows, 128), f32), shape((8, 128), f32)),
        [VMEM] * 2,
    )(sums, pair)
    gathered = lax.all_to_all(iterate, chips, 0, 0, axis_index_groups=first_groups)
    turned = kernel(
        functools.partial(transpose_kernel, copies),
        "turn",
        shape((copies, ROWS, columns), bf16),
        [VMEM],
        scratch=[pltpu.VMEM((blocks * rows, 128), f32)],
    )(gathered)
    mine = lax.all_to_all(turned, chips, 0, 0, axis_index_groups=second_groups)
    far = lax.ppermute(mine, chips, swap)
    other = lax.ppermute(mine, chips, cores)
    cost = pl.CostEstimate(flops=2 * ROWS * ROWS * columns * copies, bytes_accessed=2 * ROWS * columns * copies, transcendentals=0)
    gram_shape = shape((ROWS, ROWS), f32)
    gram, momentum_out = kernel(gram_kernel, "gram", (gram_shape, shape(grad.shape, f32)), [VMEM] * 3, cost=cost)(mine, pair, scale)
    gram = kernel(more_gram_kernel, "gram_other", gram_shape, [VMEM] * 2, cost=cost)(other, gram)
    far, gram = lax.optimization_barrier((far, gram))
    far_other = lax.ppermute(far, chips, cores)
    gram = kernel(more_gram_kernel, "gram_far", gram_shape, [VMEM] * 2, cost=cost)(far, gram)
    parts = (mine, other, far, far_other)
    update = kernel(
        functools.partial(iterate_kernel, update_scale, len(parts)),
        "newton",
        shape(grad.shape, bf16),
        [VMEM] * (len(parts) + 2),
        scratch=[
            pltpu.VMEM((ROWS, ROWS), bf16),
            pltpu.VMEM((len(parts) * copies // 2, ROWS, 2 * columns), bf16),
            pltpu.VMEM((rows, 128), f32),
            pltpu.VMEM((ROWS, ROWS), bf16),
        ],
    )(*parts, gram, own)
    return momentum_out, update


def solution(mesh):
    sizes = (4, 8, 2, 12)
    split_mesh = Mesh(mesh.devices.reshape(sizes), ("x", "y", "core", "group"))
    spec = P("group", ("x", "y", "core"), None)

    def run(grad, momentum):
        entries = grad.size
        layers, flat_rows, _ = grad.shape
        width = flat_rows * 128 // ROWS
        update_scale = 0.2 * math.sqrt(max(ROWS, width))
        return jax.shard_map(
            functools.partial(local, entries, update_scale, sizes),
            mesh=split_mesh,
            in_specs=(spec, spec),
            out_specs=(spec, spec),
            check_vma=False,
        )(grad, momentum)

    return run
```

```python
import functools
import math

import jax
import jax.numpy as jnp
import numpy as np
from jax import lax
from jax.experimental import pallas as pl
from jax.experimental.pallas import tpu as pltpu
from jax.sharding import Mesh, PartitionSpec as P

ROWS = 576
ITERS = 2

momentum_rate = 0.95
target_rms = 0.5
coef_first = 3.4445
coef_second = -4.775
coef_third = 2.0315

f32, bf16 = jnp.float32, jnp.bfloat16
VMEM = pl.BlockSpec(memory_space=pltpu.VMEM)
SMEM = pl.BlockSpec(memory_space=pltpu.SMEM)
NT = (((1,), (1,)), ((), ()))


def two_sum(a, b):
    s = a + b
    t = s - a
    return s, (a - (s - t)) + (b - t)


def fast_two_sum(a, b):
    s = a + b
    return s, b - (s - a)


def split(a):
    t = 4097.0 * a
    high = t - (t - a)
    return high, a - high


def two_prod(a, b):
    p = a * b
    ah, al = split(a)
    bh, bl = split(b)
    return p, ((ah * bh - p) + ah * bl + al * bh) + al * bl


def dd_add(a, b):
    s, e = two_sum(a[0], b[0])
    return fast_two_sum(s, e + (a[1] + b[1]))


def dd_mul(a, b):
    p, e = two_prod(a[0], b[0])
    return fast_two_sum(p, e + (a[0] * b[1] + a[1] * b[0]))


def dd_const(value):
    high = np.float32(value)
    return float(high), float(np.float32(value - float(high)))


def lazy_add(a, b):
    s, e = two_sum(a[0], b[0])
    return s, (a[1] + b[1]) + e


def tree(values):
    while len(values) > 1:
        paired = [lazy_add(values[i], values[i + 1]) for i in range(0, len(values) - 1, 2)]
        values = paired + ([values[-1]] if len(values) % 2 else [])
    return values[0]


def fold(a, axis, shifts):
    for shift in shifts:
        a = lazy_add(a, (pltpu.roll(a[0], shift, axis), pltpu.roll(a[1], shift, axis)))
    return a


def lanes():
    return lax.broadcasted_iota(jnp.int32, (8, 128), 1)


def pack(values):
    lane = lanes()
    tile = jnp.zeros((8, 128), f32)
    for i, (high, low) in enumerate(values):
        tile = jnp.where(lane == i, high, jnp.where(lane == i + 64, low, tile))
    return tile


def add_rows(ref):
    zero = jnp.zeros((8, 128), f32)
    high, low = fold(tree([(ref[i : i + 8, :], zero) for i in range(0, ref.shape[0], 8)]), 0, (4, 2, 1))
    return fast_two_sum(high, low + pltpu.roll(high, 64, 1))


def sums_kernel(pair_ref, out_ref):
    gg, gm, mm = [], [], []
    for i in range(0, pair_ref.shape[1], 8):
        g = pair_ref[0, i : i + 8, :]
        m = pair_ref[1, i : i + 8, :]
        gg.append(two_prod(g, g))
        gm.append(two_prod(g, m))
        mm.append(two_prod(m, m))
    sums = [fold(fold(tree(v), 0, (4, 2, 1)), 1, (64, 32, 16, 8, 4, 2, 1)) for v in (gg, gm, mm)]
    tile = pack([fast_two_sum(*v) for v in [sums[0]] + sums])
    for i in range(0, out_ref.shape[0], 8):
        out_ref[i : i + 8, :] = tile


def combine_kernel(groups, group_ref, in_ref, out_ref):
    high, low = add_rows(in_ref)
    lane = lanes()
    tile = jnp.where(lane < 64, high, pltpu.roll(low, 64, 1))
    for i in range(0, out_ref.shape[0], 8):
        to = lax.rem(lax.broadcasted_iota(jnp.int32, (8, 128), 0) + i, groups)
        keep = (to == group_ref[0]) | (lax.rem(lane, 64) == 0)
        out_ref[i : i + 8, :] = jnp.where(keep, tile, 0.0)


def scale_kernel(entries, in_ref, pair_ref, out_ref, own_ref, scale_ref):
    high, low = add_rows(in_ref)
    lane = lanes()

    def value(i):
        return tuple(jnp.sum(jnp.where(lane == i, v, 0.0), axis=1, keepdims=True)[0:1] for v in (high, low))

    square, gg, gm, mm = (value(i) for i in range(4))
    grad_scale = target_rms / (jnp.sqrt(square[0] / entries) + 1e-06)
    rate = float(np.float32(momentum_rate))
    factor_high, factor_low = dd_const(1.0 + rate)
    ones = jnp.ones_like(grad_scale)
    a = two_prod(grad_scale, factor_high * ones)
    a = fast_two_sum(a[0], a[1] + grad_scale * factor_low)
    b = tuple(v * ones for v in dd_const(rate * rate))
    cross = dd_mul(dd_mul((2.0 * a[0], 2.0 * a[1]), b), gm)
    total = dd_add(dd_add(dd_mul(a, dd_mul(a, gg)), dd_mul(dd_mul(b, b), mm)), cross)
    unorm = jnp.sqrt(jnp.maximum(total[0], 0.0))
    scaled_grad = grad_scale * pair_ref[0]
    nudged = scaled_grad + momentum_rate * (momentum_rate * pair_ref[1] + scaled_grad)
    iterate = (nudged / (unorm + 1e-07)).astype(bf16)
    for i in range(out_ref.shape[0]):
        out_ref[i] = iterate
    own_ref[...] = iterate.astype(f32)
    scale_ref[...] = jnp.broadcast_to(grad_scale, scale_ref.shape)


def transpose_kernel(copies, in_ref, out_ref, flat_ref):
    blocks, rows = in_ref.shape[:2]
    for i in range(blocks):
        flat_ref[i * rows : (i + 1) * rows, :] = in_ref[i].astype(f32)
    half = blocks * rows // 9
    for j in range(9):
        turned = flat_ref[pl.ds(j, half, stride=9), :].T.astype(bf16)
        for i in range(copies):
            if j < 4:
                out_ref[i, 128 * j : 128 * j + 128, 0:half] = turned
            elif j == 4:
                out_ref[i, 512:576, 0:half] = turned[0:64]
                out_ref[i, 0:64, half : 2 * half] = turned[64:128]
            else:
                out_ref[i, 128 * j - 576 : 128 * j - 448, half : 2 * half] = turned


def own_load(flat_ref, pairs):
    low = lax.broadcasted_iota(jnp.int32, (pairs, 128), 1) < 64
    flat = [flat_ref[pl.ds(j, pairs, stride=9), :] for j in range(9)]
    turned = [pltpu.roll(flat[j], 64, 1) for j in range(4, 9)]
    even = flat[:4] + [flat[4]]
    odd = [jnp.where(low, turned[k], turned[k + 1]) for k in range(4)] + [turned[4]]
    return jnp.concatenate([jnp.concatenate(even, 1), jnp.concatenate(odd, 1)], 0)[:, :ROWS]


def own_store(flat_ref, value, pairs):
    value = jnp.concatenate([value, jnp.zeros((2 * pairs, 64), f32)], 1)
    low = lax.broadcasted_iota(jnp.int32, (pairs, 128), 1) < 64
    even = [value[:pairs, 128 * j : 128 * j + 128] for j in range(5)]
    odd = [pltpu.roll(value[pairs:, 128 * j : 128 * j + 128], 64, 1) for j in range(5)]
    flat = even[:4] + [jnp.where(low, even[4], odd[0])]
    flat += [jnp.where(low, odd[k], odd[k + 1]) for k in range(4)]
    for j in range(9):
        flat_ref[pl.ds(j, pairs, stride=9), :] = flat[j]


def triangle():
    return [(a, min(a + 256, ROWS)) for a in range(0, ROWS, 256)]


def side_by_side(values):
    return jnp.concatenate(values, 1)


def gram_columns(iterate):
    return [lax.dot_general(iterate[a:], iterate[a:b], NT, preferred_element_type=f32) for a, b in triangle()]


def mirror(ref, value, a, b):
    ref[a:, a:b] = value
    if b < ROWS:
        ref[a:b, b:] = value[b - a :].T


def store_poly(columns, low_ref, poly_ref):
    for (a, b), column in zip(triangle(), columns):
        mirror(low_ref, column.astype(bf16), a, b)
    for (a, b), column in zip(triangle(), columns):
        squared = jnp.dot(low_ref[a:, :], low_ref[:, a:b], preferred_element_type=f32)
        mirror(poly_ref, (coef_second * column + coef_third * squared).astype(bf16), a, b)


def gram_kernel(mine_ref, pair_ref, scale_ref, gram_ref, momentum_out_ref):
    iterate = side_by_side([mine_ref[i] for i in range(mine_ref.shape[0])])
    for (a, b), column in zip(triangle(), gram_columns(iterate)):
        gram_ref[a:, a:b] = column
    momentum_out_ref[0] = momentum_rate * pair_ref[1] + scale_ref[0:1, :] * pair_ref[0]


def iterate_kernel(update_scale, mine_ref, other_ref, gram_ref, own_ref, out_ref, poly_ref, next_ref, flat_ref, low_ref):
    blocks = [side_by_side([r[i], r[i + 1]]) for r in (mine_ref, other_ref) for i in range(0, r.shape[0], 2)]
    pairs = own_ref.shape[0] // 9
    columns = gram_columns(side_by_side([other_ref[i] for i in range(other_ref.shape[0])]))
    columns = [gram_ref[a:, a:b] + column for (a, b), column in zip(triangle(), columns)]
    store_poly(columns, low_ref, poly_ref)
    for i, v in enumerate(blocks):
        product = jnp.dot(poly_ref[...], v, preferred_element_type=f32)
        next_ref[i] = (coef_first * v.astype(f32) + product).astype(bf16)
    columns = gram_columns(side_by_side([next_ref[i] for i in range(len(blocks))]))
    own = own_load(own_ref, pairs)
    product = jnp.dot(own.astype(bf16), poly_ref[...], preferred_element_type=f32)
    own = (coef_first * own + product).astype(bf16)
    store_poly(columns, low_ref, poly_ref)
    product = side_by_side([jnp.dot(own, poly_ref[:, a:b], preferred_element_type=f32) for a, b in triangle()])
    own_store(flat_ref, update_scale * (coef_first * own.astype(f32) + product), pairs)
    out_ref[0] = flat_ref[...].astype(bf16)


def pairings(count, core):
    return [((i + core) % count, (i + core + 1) % count) for i in range(0, count, 2)]


def gather_groups(nx, ny, nc):
    def at(x, y, core):
        return (x * ny + y) * nc + core

    first, second = [], []
    for core in range(nc):
        for x in range(nx):
            first += [[at(x, y, core) for y in range(parity, ny, 2)] for parity in range(2)]
        second += [[at(x, y, core) for x in range(nx) for y in ys] for ys in pairings(ny, core)]
    return first, second


def kernel(body, name, out, in_specs, scratch=(), cost=None):
    return pl.pallas_call(
        body,
        name=name,
        out_shape=out,
        in_specs=in_specs,
        out_specs=jax.tree.map(lambda _: VMEM, out),
        scratch_shapes=list(scratch),
        compiler_params=pltpu.CompilerParams(vmem_limit_bytes=40 * 2**20),
        cost_estimate=cost,
    )


def local(entries, update_scale, sizes, grad, momentum):
    nx, ny, nc, ng = sizes
    chips = ("x", "y", "core")
    first_groups, second_groups = gather_groups(nx, ny, nc)
    blocks, copies = len(first_groups[0]), len(second_groups[0])
    rows = grad.shape[1]
    columns = blocks * rows * 128 // ROWS
    shape = jax.ShapeDtypeStruct
    group = lax.axis_index("group").astype(jnp.int32).reshape(1)
    grad, momentum, group = lax.optimization_barrier((grad, momentum, group))
    first = lax.broadcasted_iota(jnp.int32, (2, rows, 128), 0) == 0
    pair = jnp.where(first, grad, momentum)
    sums = kernel(sums_kernel, "sums", shape((ny * nc, 128), f32), [VMEM])(pair)
    sums = lax.all_to_all(sums.reshape(-1, 1, 128), ("y", "core"), 0, 0).reshape(-1, 128)
    sums = kernel(functools.partial(combine_kernel, ng), "combine", shape((nx * ng, 128), f32), [SMEM, VMEM])(group, sums)
    sums = lax.all_to_all(sums.reshape(-1, 1, 128), ("x", "group"), 0, 0).reshape(-1, 128)
    iterate, own, scale = kernel(
        functools.partial(scale_kernel, entries),
        "scale",
        (shape((blocks, rows, 128), bf16), shape((rows, 128), f32), shape((8, 128), f32)),
        [VMEM] * 2,
    )(sums, pair)
    gathered = lax.all_to_all(iterate, chips, 0, 0, axis_index_groups=first_groups)
    turned = kernel(
        functools.partial(transpose_kernel, copies),
        "turn",
        shape((copies, ROWS, columns), bf16),
        [VMEM],
        scratch=[pltpu.VMEM((blocks * rows, 128), f32)],
    )(gathered)
    mine = lax.all_to_all(turned, chips, 0, 0, axis_index_groups=second_groups)
    other = lax.ppermute(mine, "core", [(0, 1), (1, 0)])
    gram, momentum_out = kernel(
        gram_kernel,
        "gram",
        (shape((ROWS, ROWS), f32), shape(grad.shape, f32)),
        [VMEM] * 3,
        cost=pl.CostEstimate(flops=2 * ROWS * ROWS * columns * copies, bytes_accessed=2 * ROWS * columns * copies, transcendentals=0),
    )(mine, pair, scale)
    update = kernel(
        functools.partial(iterate_kernel, update_scale),
        "newton",
        shape(grad.shape, bf16),
        [VMEM] * 4,
        scratch=[
            pltpu.VMEM((ROWS, ROWS), bf16),
            pltpu.VMEM((copies, ROWS, 2 * columns), bf16),
            pltpu.VMEM((rows, 128), f32),
            pltpu.VMEM((ROWS, ROWS), bf16),
        ],
    )(mine, other, gram, own)
    return momentum_out, update


def solution(mesh):
    sizes = (4, 8, 2, 12)
    split_mesh = Mesh(mesh.devices.reshape(sizes), ("x", "y", "core", "group"))
    spec = P("group", ("x", "y", "core"), None)

    def run(grad, momentum):
        entries = grad.size
        layers, flat_rows, _ = grad.shape
        width = flat_rows * 128 // ROWS
        update_scale = 0.2 * math.sqrt(max(ROWS, width))
        return jax.shard_map(
            functools.partial(local, entries, update_scale, sizes),
            mesh=split_mesh,
            in_specs=(spec, spec),
            out_specs=(spec, spec),
            check_vma=False,
        )(grad, momentum)

    return run
```

```python
import functools
import math

import jax
import jax.numpy as jnp
import numpy as np
from jax import lax
from jax.experimental import pallas as pl
from jax.experimental.pallas import tpu as pltpu
from jax.sharding import Mesh, PartitionSpec as P

ROWS = 576
ITERS = 2

momentum_rate = 0.95
target_rms = 0.5
coef_first = 3.4445
coef_second = -4.775
coef_third = 2.0315

f32, bf16 = jnp.float32, jnp.bfloat16
VMEM = pl.BlockSpec(memory_space=pltpu.VMEM)
SMEM = pl.BlockSpec(memory_space=pltpu.SMEM)
NT = (((1,), (1,)), ((), ()))


def two_sum(a, b):
    s = a + b
    t = s - a
    return s, (a - (s - t)) + (b - t)


def fast_two_sum(a, b):
    s = a + b
    return s, b - (s - a)


def split(a):
    t = 4097.0 * a
    high = t - (t - a)
    return high, a - high


def two_prod(a, b):
    p = a * b
    ah, al = split(a)
    bh, bl = split(b)
    return p, ((ah * bh - p) + ah * bl + al * bh) + al * bl


def dd_add(a, b):
    s, e = two_sum(a[0], b[0])
    return fast_two_sum(s, e + (a[1] + b[1]))


def dd_mul(a, b):
    p, e = two_prod(a[0], b[0])
    return fast_two_sum(p, e + (a[0] * b[1] + a[1] * b[0]))


def dd_const(value):
    high = np.float32(value)
    return float(high), float(np.float32(value - float(high)))


def lazy_add(a, b):
    s, e = two_sum(a[0], b[0])
    return s, (a[1] + b[1]) + e


def tree(values):
    while len(values) > 1:
        paired = [lazy_add(values[i], values[i + 1]) for i in range(0, len(values) - 1, 2)]
        values = paired + ([values[-1]] if len(values) % 2 else [])
    return values[0]


def fold(a, axis, shifts):
    for shift in shifts:
        a = lazy_add(a, (pltpu.roll(a[0], shift, axis), pltpu.roll(a[1], shift, axis)))
    return a


def lanes():
    return lax.broadcasted_iota(jnp.int32, (8, 128), 1)


def pack(values):
    lane = lanes()
    tile = jnp.zeros((8, 128), f32)
    for i, (high, low) in enumerate(values):
        tile = jnp.where(lane == i, high, jnp.where(lane == i + 64, low, tile))
    return tile


def add_rows(ref):
    zero = jnp.zeros((8, 128), f32)
    high, low = fold(tree([(ref[i : i + 8, :], zero) for i in range(0, ref.shape[0], 8)]), 0, (4, 2, 1))
    return fast_two_sum(high, low + pltpu.roll(high, 64, 1))


def sums_kernel(pair_ref, out_ref):
    gg, gm, mm = [], [], []
    for i in range(0, pair_ref.shape[1], 8):
        g = pair_ref[0, i : i + 8, :]
        m = pair_ref[1, i : i + 8, :]
        gg.append(two_prod(g, g))
        gm.append(two_prod(g, m))
        mm.append(two_prod(m, m))
    sums = [fold(fold(tree(v), 0, (4, 2, 1)), 1, (64, 32, 16, 8, 4, 2, 1)) for v in (gg, gm, mm)]
    tile = pack([fast_two_sum(*v) for v in [sums[0]] + sums])
    for i in range(0, out_ref.shape[0], 8):
        out_ref[i : i + 8, :] = tile


def combine_kernel(groups, group_ref, in_ref, out_ref):
    high, low = add_rows(in_ref)
    lane = lanes()
    tile = jnp.where(lane < 64, high, pltpu.roll(low, 64, 1))
    for i in range(0, out_ref.shape[0], 8):
        to = lax.rem(lax.broadcasted_iota(jnp.int32, (8, 128), 0) + i, groups)
        keep = (to == group_ref[0]) | (lax.rem(lane, 64) == 0)
        out_ref[i : i + 8, :] = jnp.where(keep, tile, 0.0)


def scale_kernel(entries, in_ref, pair_ref, out_ref, own_ref, scale_ref):
    high, low = add_rows(in_ref)
    lane = lanes()

    def value(i):
        return tuple(jnp.sum(jnp.where(lane == i, v, 0.0), axis=1, keepdims=True)[0:1] for v in (high, low))

    square, gg, gm, mm = (value(i) for i in range(4))
    grad_scale = target_rms / (jnp.sqrt(square[0] / entries) + 1e-06)
    rate = float(np.float32(momentum_rate))
    factor_high, factor_low = dd_const(1.0 + rate)
    ones = jnp.ones_like(grad_scale)
    a = two_prod(grad_scale, factor_high * ones)
    a = fast_two_sum(a[0], a[1] + grad_scale * factor_low)
    b = tuple(v * ones for v in dd_const(rate * rate))
    cross = dd_mul(dd_mul((2.0 * a[0], 2.0 * a[1]), b), gm)
    total = dd_add(dd_add(dd_mul(a, dd_mul(a, gg)), dd_mul(dd_mul(b, b), mm)), cross)
    unorm = jnp.sqrt(jnp.maximum(total[0], 0.0))
    scaled_grad = grad_scale * pair_ref[0]
    nudged = scaled_grad + momentum_rate * (momentum_rate * pair_ref[1] + scaled_grad)
    iterate = (nudged / (unorm + 1e-07)).astype(bf16)
    for i in range(out_ref.shape[0]):
        out_ref[i] = iterate
    own_ref[...] = iterate.astype(f32)
    scale_ref[...] = jnp.broadcast_to(grad_scale, scale_ref.shape)


def transpose_kernel(copies, in_ref, out_ref, flat_ref):
    blocks, rows = in_ref.shape[:2]
    for i in range(blocks):
        flat_ref[i * rows : (i + 1) * rows, :] = in_ref[i].astype(f32)
    half = blocks * rows // 9
    low = lax.broadcasted_iota(jnp.int32, (half, 128), 1) < 64
    flat = [flat_ref[pl.ds(j, half, stride=9), :] for j in range(9)]
    turned = [pltpu.roll(flat[j], 64, 1) for j in range(4, 9)]
    for j in range(5):
        odd = jnp.where(low, turned[j], turned[j + 1]) if j < 4 else turned[4]
        block = jnp.concatenate([flat[j], odd], 0).T.astype(bf16)
        width = min(128, ROWS - 128 * j)
        for i in range(copies):
            out_ref[i, 128 * j : 128 * j + width, :] = block[:width]


def own_load(flat_ref, pairs):
    low = lax.broadcasted_iota(jnp.int32, (pairs, 128), 1) < 64
    flat = [flat_ref[pl.ds(j, pairs, stride=9), :] for j in range(9)]
    turned = [pltpu.roll(flat[j], 64, 1) for j in range(4, 9)]
    even = flat[:4] + [flat[4]]
    odd = [jnp.where(low, turned[k], turned[k + 1]) for k in range(4)] + [turned[4]]
    return jnp.concatenate([jnp.concatenate(even, 1), jnp.concatenate(odd, 1)], 0)[:, :ROWS]


def own_store(flat_ref, value, pairs):
    value = jnp.concatenate([value, jnp.zeros((2 * pairs, 64), f32)], 1)
    low = lax.broadcasted_iota(jnp.int32, (pairs, 128), 1) < 64
    even = [value[:pairs, 128 * j : 128 * j + 128] for j in range(5)]
    odd = [pltpu.roll(value[pairs:, 128 * j : 128 * j + 128], 64, 1) for j in range(5)]
    flat = even[:4] + [jnp.where(low, even[4], odd[0])]
    flat += [jnp.where(low, odd[k], odd[k + 1]) for k in range(4)]
    for j in range(9):
        flat_ref[pl.ds(j, pairs, stride=9), :] = flat[j]


def triangle():
    return [(a, min(a + 256, ROWS)) for a in range(0, ROWS, 256)]


def side_by_side(values):
    return jnp.concatenate(values, 1)


def gram_columns(iterate):
    return [lax.dot_general(iterate[a:], iterate[a:b], NT, preferred_element_type=f32) for a, b in triangle()]


def mirror(ref, value, a, b):
    ref[a:, a:b] = value
    if b < ROWS:
        ref[a:b, b:] = value[b - a :].T


def store_poly(columns, low_ref, poly_ref):
    for (a, b), column in zip(triangle(), columns):
        mirror(low_ref, column.astype(bf16), a, b)
    for (a, b), column in zip(triangle(), columns):
        squared = jnp.dot(low_ref[a:, :], low_ref[:, a:b], preferred_element_type=f32)
        mirror(poly_ref, (coef_second * column + coef_third * squared).astype(bf16), a, b)


def gram_kernel(mine_ref, pair_ref, scale_ref, gram_ref, momentum_out_ref):
    iterate = side_by_side([mine_ref[i] for i in range(mine_ref.shape[0])])
    for (a, b), column in zip(triangle(), gram_columns(iterate)):
        gram_ref[a:, a:b] = column
    momentum_out_ref[0] = momentum_rate * pair_ref[1] + scale_ref[0:1, :] * pair_ref[0]


def iterate_kernel(update_scale, mine_ref, other_ref, gram_ref, own_ref, out_ref, poly_ref, next_ref, flat_ref, low_ref):
    blocks = [side_by_side([r[i], r[i + 1]]) for r in (mine_ref, other_ref) for i in range(0, r.shape[0], 2)]
    pairs = own_ref.shape[0] // 9
    columns = gram_columns(side_by_side([other_ref[i] for i in range(other_ref.shape[0])]))
    columns = [gram_ref[a:, a:b] + column for (a, b), column in zip(triangle(), columns)]
    store_poly(columns, low_ref, poly_ref)
    for i, v in enumerate(blocks):
        product = jnp.dot(poly_ref[...], v, preferred_element_type=f32)
        next_ref[i] = (coef_first * v.astype(f32) + product).astype(bf16)
    columns = gram_columns(side_by_side([next_ref[i] for i in range(len(blocks))]))
    own = own_load(own_ref, pairs)
    product = jnp.dot(own.astype(bf16), poly_ref[...], preferred_element_type=f32)
    own = (coef_first * own + product).astype(bf16)
    store_poly(columns, low_ref, poly_ref)
    product = side_by_side([jnp.dot(own, poly_ref[:, a:b], preferred_element_type=f32) for a, b in triangle()])
    own_store(flat_ref, update_scale * (coef_first * own.astype(f32) + product), pairs)
    out_ref[0] = flat_ref[...].astype(bf16)


def pairings(count, core):
    return [((i + core) % count, (i + core + 1) % count) for i in range(0, count, 2)]


def gather_groups(nx, ny, nc):
    def at(x, y, core):
        return (x * ny + y) * nc + core

    first, second = [], []
    for core in range(nc):
        for x in range(nx):
            first += [[at(x, y, core) for y in range(parity, ny, 2)] for parity in range(2)]
        second += [[at(x, y, core) for x in range(nx) for y in ys] for ys in pairings(ny, 0)]
    return first, second


def kernel(body, name, out, in_specs, scratch=(), cost=None):
    return pl.pallas_call(
        body,
        name=name,
        out_shape=out,
        in_specs=in_specs,
        out_specs=jax.tree.map(lambda _: VMEM, out),
        scratch_shapes=list(scratch),
        compiler_params=pltpu.CompilerParams(vmem_limit_bytes=40 * 2**20),
        cost_estimate=cost,
    )


def local(entries, update_scale, sizes, grad, momentum):
    nx, ny, nc, ng = sizes
    chips = ("x", "y", "core")
    first_groups, second_groups = gather_groups(nx, ny, nc)
    blocks, copies = len(first_groups[0]), len(second_groups[0])
    rows = grad.shape[1]
    columns = blocks * rows * 128 // ROWS
    shape = jax.ShapeDtypeStruct
    group = lax.axis_index("group").astype(jnp.int32).reshape(1)
    grad, momentum, group = lax.optimization_barrier((grad, momentum, group))
    first = lax.broadcasted_iota(jnp.int32, (2, rows, 128), 0) == 0
    pair = jnp.where(first, grad, momentum)
    sums = kernel(sums_kernel, "sums", shape((ny * nc, 128), f32), [VMEM])(pair)
    sums = lax.all_to_all(sums.reshape(-1, 1, 128), ("y", "core"), 0, 0).reshape(-1, 128)
    sums = kernel(functools.partial(combine_kernel, ng), "combine", shape((nx * ng, 128), f32), [SMEM, VMEM])(group, sums)
    sums = lax.all_to_all(sums.reshape(-1, 1, 128), ("x", "group"), 0, 0).reshape(-1, 128)
    iterate, own, scale = kernel(
        functools.partial(scale_kernel, entries),
        "scale",
        (shape((blocks, rows, 128), bf16), shape((rows, 128), f32), shape((8, 128), f32)),
        [VMEM] * 2,
    )(sums, pair)
    gathered = lax.all_to_all(iterate, chips, 0, 0, axis_index_groups=first_groups)
    turned = kernel(
        functools.partial(transpose_kernel, copies),
        "turn",
        shape((copies, ROWS, columns), bf16),
        [VMEM],
        scratch=[pltpu.VMEM((blocks * rows, 128), f32)],
    )(gathered)
    mine = lax.all_to_all(turned, chips, 0, 0, axis_index_groups=second_groups)
    other = lax.ppermute(mine, "core", [(0, 1), (1, 0)])
    gram, momentum_out = kernel(
        gram_kernel,
        "gram",
        (shape((ROWS, ROWS), f32), shape(grad.shape, f32)),
        [VMEM] * 3,
        cost=pl.CostEstimate(flops=2 * ROWS * ROWS * columns * copies, bytes_accessed=2 * ROWS * columns * copies, transcendentals=0),
    )(mine, pair, scale)
    update = kernel(
        functools.partial(iterate_kernel, update_scale),
        "newton",
        shape(grad.shape, bf16),
        [VMEM] * 4,
        scratch=[
            pltpu.VMEM((ROWS, ROWS), bf16),
            pltpu.VMEM((copies, ROWS, 2 * columns), bf16),
            pltpu.VMEM((rows, 128), f32),
            pltpu.VMEM((ROWS, ROWS), bf16),
        ],
    )(mine, other, gram, own)
    return momentum_out, update


def solution(mesh):
    sizes = (4, 8, 2, 12)
    split_mesh = Mesh(mesh.devices.reshape(sizes), ("x", "y", "core", "group"))
    spec = P("group", ("x", "y", "core"), None)

    def run(grad, momentum):
        entries = grad.size
        layers, flat_rows, _ = grad.shape
        width = flat_rows * 128 // ROWS
        update_scale = 0.2 * math.sqrt(max(ROWS, width))
        return jax.shard_map(
            functools.partial(local, entries, update_scale, sizes),
            mesh=split_mesh,
            in_specs=(spec, spec),
            out_specs=(spec, spec),
            check_vma=False,
        )(grad, momentum)

    return run
```

```python
import functools
import math

import jax
import jax.numpy as jnp
import numpy as np
from jax import lax
from jax.experimental import pallas as pl
from jax.experimental.pallas import tpu as pltpu
from jax.sharding import Mesh, PartitionSpec as P

ROWS = 576
ITERS = 2

momentum_rate = 0.95
target_rms = 0.5
coef_first = 3.4445
coef_second = -4.775
coef_third = 2.0315

f32, bf16 = jnp.float32, jnp.bfloat16
VMEM = pl.BlockSpec(memory_space=pltpu.VMEM)
SMEM = pl.BlockSpec(memory_space=pltpu.SMEM)
NT = (((1,), (1,)), ((), ()))


def two_sum(a, b):
    s = a + b
    t = s - a
    return s, (a - (s - t)) + (b - t)


def fast_two_sum(a, b):
    s = a + b
    return s, b - (s - a)


def split(a):
    t = 4097.0 * a
    high = t - (t - a)
    return high, a - high


def two_prod(a, b):
    p = a * b
    ah, al = split(a)
    bh, bl = split(b)
    return p, ((ah * bh - p) + ah * bl + al * bh) + al * bl


def dd_add(a, b):
    s, e = two_sum(a[0], b[0])
    return fast_two_sum(s, e + (a[1] + b[1]))


def dd_mul(a, b):
    p, e = two_prod(a[0], b[0])
    return fast_two_sum(p, e + (a[0] * b[1] + a[1] * b[0]))


def dd_const(value):
    high = np.float32(value)
    return float(high), float(np.float32(value - float(high)))


def lazy_add(a, b):
    s, e = two_sum(a[0], b[0])
    return s, (a[1] + b[1]) + e


def tree(values):
    while len(values) > 1:
        paired = [lazy_add(values[i], values[i + 1]) for i in range(0, len(values) - 1, 2)]
        values = paired + ([values[-1]] if len(values) % 2 else [])
    return values[0]


def fold(a, axis, shifts):
    for shift in shifts:
        a = lazy_add(a, (pltpu.roll(a[0], shift, axis), pltpu.roll(a[1], shift, axis)))
    return a


def lanes():
    return lax.broadcasted_iota(jnp.int32, (8, 128), 1)


def pack(values):
    lane = lanes()
    tile = jnp.zeros((8, 128), f32)
    for i, (high, low) in enumerate(values):
        tile = jnp.where(lane == i, high, jnp.where(lane == i + 64, low, tile))
    return tile


def add_rows(ref):
    zero = jnp.zeros((8, 128), f32)
    high, low = fold(tree([(ref[i : i + 8, :], zero) for i in range(0, ref.shape[0], 8)]), 0, (4, 2, 1))
    return fast_two_sum(high, low + pltpu.roll(high, 64, 1))


def sums_kernel(pair_ref, out_ref):
    gg, gm, mm = [], [], []
    for i in range(0, pair_ref.shape[1], 8):
        g = pair_ref[0, i : i + 8, :]
        m = pair_ref[1, i : i + 8, :]
        gg.append(two_prod(g, g))
        gm.append(two_prod(g, m))
        mm.append(two_prod(m, m))
    sums = [fold(fold(tree(v), 0, (4, 2, 1)), 1, (64, 32, 16, 8, 4, 2, 1)) for v in (gg, gm, mm)]
    tile = pack([fast_two_sum(*v) for v in [sums[0]] + sums])
    for i in range(0, out_ref.shape[0], 8):
        out_ref[i : i + 8, :] = tile


def combine_kernel(groups, group_ref, in_ref, out_ref):
    high, low = add_rows(in_ref)
    lane = lanes()
    tile = jnp.where(lane < 64, high, pltpu.roll(low, 64, 1))
    for i in range(0, out_ref.shape[0], 8):
        to = lax.rem(lax.broadcasted_iota(jnp.int32, (8, 128), 0) + i, groups)
        keep = (to == group_ref[0]) | (lax.rem(lane, 64) == 0)
        out_ref[i : i + 8, :] = jnp.where(keep, tile, 0.0)


def scale_kernel(entries, in_ref, pair_ref, out_ref, own_ref, scale_ref):
    high, low = add_rows(in_ref)
    lane = lanes()

    def value(i):
        return tuple(jnp.sum(jnp.where(lane == i, v, 0.0), axis=1, keepdims=True)[0:1] for v in (high, low))

    square, gg, gm, mm = (value(i) for i in range(4))
    grad_scale = target_rms / (jnp.sqrt(square[0] / entries) + 1e-06)
    rate = float(np.float32(momentum_rate))
    factor_high, factor_low = dd_const(1.0 + rate)
    ones = jnp.ones_like(grad_scale)
    a = two_prod(grad_scale, factor_high * ones)
    a = fast_two_sum(a[0], a[1] + grad_scale * factor_low)
    b = tuple(v * ones for v in dd_const(rate * rate))
    cross = dd_mul(dd_mul((2.0 * a[0], 2.0 * a[1]), b), gm)
    total = dd_add(dd_add(dd_mul(a, dd_mul(a, gg)), dd_mul(dd_mul(b, b), mm)), cross)
    unorm = jnp.sqrt(jnp.maximum(total[0], 0.0))
    scaled_grad = grad_scale * pair_ref[0]
    nudged = scaled_grad + momentum_rate * (momentum_rate * pair_ref[1] + scaled_grad)
    iterate = (nudged / (unorm + 1e-07)).astype(bf16)
    for i in range(out_ref.shape[0]):
        out_ref[i] = iterate
    own_ref[...] = iterate.astype(f32)
    scale_ref[...] = jnp.broadcast_to(grad_scale, scale_ref.shape)


def transpose_kernel(copies, in_ref, out_ref, flat_ref):
    blocks, rows = in_ref.shape[:2]
    for i in range(blocks):
        flat_ref[i * rows : (i + 1) * rows, :] = in_ref[i].astype(f32)
    half = blocks * rows // 9
    low = lax.broadcasted_iota(jnp.int32, (half, 128), 1) < 64
    flat = [flat_ref[pl.ds(j, half, stride=9), :] for j in range(9)]
    turned = [pltpu.roll(flat[j], 64, 1) for j in range(4, 9)]
    for j in range(5):
        odd = jnp.where(low, turned[j], turned[j + 1]) if j < 4 else turned[4]
        block = jnp.concatenate([flat[j], odd], 0).T.astype(bf16)
        width = min(128, ROWS - 128 * j)
        for i in range(copies):
            out_ref[i, 128 * j : 128 * j + width, :] = block[:width]


def own_load(flat_ref, pairs):
    low = lax.broadcasted_iota(jnp.int32, (pairs, 128), 1) < 64
    flat = [flat_ref[pl.ds(j, pairs, stride=9), :] for j in range(9)]
    turned = [pltpu.roll(flat[j], 64, 1) for j in range(4, 9)]
    even = flat[:4] + [flat[4]]
    odd = [jnp.where(low, turned[k], turned[k + 1]) for k in range(4)] + [turned[4]]
    return jnp.concatenate([jnp.concatenate(even, 1), jnp.concatenate(odd, 1)], 0)[:, :ROWS]


def own_store(flat_ref, value, pairs):
    value = jnp.concatenate([value, jnp.zeros((2 * pairs, 64), f32)], 1)
    low = lax.broadcasted_iota(jnp.int32, (pairs, 128), 1) < 64
    even = [value[:pairs, 128 * j : 128 * j + 128] for j in range(5)]
    odd = [pltpu.roll(value[pairs:, 128 * j : 128 * j + 128], 64, 1) for j in range(5)]
    flat = even[:4] + [jnp.where(low, even[4], odd[0])]
    flat += [jnp.where(low, odd[k], odd[k + 1]) for k in range(4)]
    for j in range(9):
        flat_ref[pl.ds(j, pairs, stride=9), :] = flat[j]


def triangle():
    return [(a, min(a + 256, ROWS)) for a in range(0, ROWS, 256)]


def side_by_side(values):
    return jnp.concatenate(values, 1)


def gram_columns(iterate):
    return [lax.dot_general(iterate[a:], iterate[a:b], NT, preferred_element_type=f32) for a, b in triangle()]


def mirror(ref, value, a, b):
    ref[a:, a:b] = value
    if b < ROWS:
        ref[a:b, b:] = value[b - a :].T


def store_poly(columns, low_ref, poly_ref):
    for (a, b), column in zip(triangle(), columns):
        mirror(low_ref, column.astype(bf16), a, b)
    for (a, b), column in zip(triangle(), columns):
        squared = jnp.dot(low_ref[a:, :], low_ref[:, a:b], preferred_element_type=f32)
        mirror(poly_ref, (coef_second * column + coef_third * squared).astype(bf16), a, b)


def gram_kernel(mine_ref, pair_ref, scale_ref, gram_ref, momentum_out_ref):
    iterate = side_by_side([mine_ref[i] for i in range(mine_ref.shape[0])])
    for (a, b), column in zip(triangle(), gram_columns(iterate)):
        gram_ref[a:, a:b] = column
    momentum_out_ref[0] = momentum_rate * pair_ref[1] + scale_ref[0:1, :] * pair_ref[0]


def iterate_kernel(update_scale, mine_ref, other_ref, gram_ref, own_ref, out_ref, poly_ref, next_ref, flat_ref, low_ref):
    blocks = [side_by_side([r[i], r[i + 1]]) for r in (mine_ref, other_ref) for i in range(0, r.shape[0], 2)]
    pairs = own_ref.shape[0] // 9
    columns = gram_columns(side_by_side([other_ref[i] for i in range(other_ref.shape[0])]))
    columns = [gram_ref[a:, a:b] + column for (a, b), column in zip(triangle(), columns)]
    store_poly(columns, low_ref, poly_ref)
    for i, v in enumerate(blocks):
        product = jnp.dot(poly_ref[...], v, preferred_element_type=f32)
        next_ref[i] = (coef_first * v.astype(f32) + product).astype(bf16)
    columns = gram_columns(side_by_side([next_ref[i] for i in range(len(blocks))]))
    own = own_load(own_ref, pairs)
    product = jnp.dot(own.astype(bf16), poly_ref[...], preferred_element_type=f32)
    own = (coef_first * own + product).astype(bf16)
    store_poly(columns, low_ref, poly_ref)
    product = side_by_side([jnp.dot(own, poly_ref[:, a:b], preferred_element_type=f32) for a, b in triangle()])
    own_store(flat_ref, update_scale * (coef_first * own.astype(f32) + product), pairs)
    out_ref[0] = flat_ref[...].astype(bf16)


def pairings(count, core):
    return [((i + core) % count, (i + core + 1) % count) for i in range(0, count, 2)]


def gather_groups(nx, ny, nc):
    def at(x, y, core):
        return (x * ny + y) * nc + core

    first, second = [], []
    for core in range(nc):
        for x in range(nx):
            first += [[at(x, y, core) for y in range(parity, ny, 2)] for parity in range(2)]
        second += [[at(x, y, core) for y in ys for x in range(nx)] for ys in pairings(ny, 0)]
    return first, second


def kernel(body, name, out, in_specs, scratch=(), cost=None):
    return pl.pallas_call(
        body,
        name=name,
        out_shape=out,
        in_specs=in_specs,
        out_specs=jax.tree.map(lambda _: VMEM, out),
        scratch_shapes=list(scratch),
        compiler_params=pltpu.CompilerParams(vmem_limit_bytes=40 * 2**20),
        cost_estimate=cost,
    )


def local(entries, update_scale, sizes, grad, momentum):
    nx, ny, nc, ng = sizes
    chips = ("x", "y", "core")
    first_groups, second_groups = gather_groups(nx, ny, nc)
    blocks, copies = len(first_groups[0]), len(second_groups[0])
    rows = grad.shape[1]
    columns = blocks * rows * 128 // ROWS
    shape = jax.ShapeDtypeStruct
    group = lax.axis_index("group").astype(jnp.int32).reshape(1)
    grad, momentum, group = lax.optimization_barrier((grad, momentum, group))
    first = lax.broadcasted_iota(jnp.int32, (2, rows, 128), 0) == 0
    pair = jnp.where(first, grad, momentum)
    sums = kernel(sums_kernel, "sums", shape((ny * nc, 128), f32), [VMEM])(pair)
    sums = lax.all_to_all(sums.reshape(-1, 1, 128), ("y", "core"), 0, 0).reshape(-1, 128)
    sums = kernel(functools.partial(combine_kernel, ng), "combine", shape((nx * ng, 128), f32), [SMEM, VMEM])(group, sums)
    sums = lax.all_to_all(sums.reshape(-1, 1, 128), ("x", "group"), 0, 0).reshape(-1, 128)
    iterate, own, scale = kernel(
        functools.partial(scale_kernel, entries),
        "scale",
        (shape((blocks, rows, 128), bf16), shape((rows, 128), f32), shape((8, 128), f32)),
        [VMEM] * 2,
    )(sums, pair)
    gathered = lax.all_to_all(iterate, chips, 0, 0, axis_index_groups=first_groups)
    turned = kernel(
        functools.partial(transpose_kernel, copies),
        "turn",
        shape((copies, ROWS, columns), bf16),
        [VMEM],
        scratch=[pltpu.VMEM((blocks * rows, 128), f32)],
    )(gathered)
    mine = lax.all_to_all(turned, chips, 0, 0, axis_index_groups=second_groups)
    other = lax.ppermute(mine, "core", [(0, 1), (1, 0)])
    gram, momentum_out = kernel(
        gram_kernel,
        "gram",
        (shape((ROWS, ROWS), f32), shape(grad.shape, f32)),
        [VMEM] * 3,
        cost=pl.CostEstimate(flops=2 * ROWS * ROWS * columns * copies, bytes_accessed=2 * ROWS * columns * copies, transcendentals=0),
    )(mine, pair, scale)
    update = kernel(
        functools.partial(iterate_kernel, update_scale),
        "newton",
        shape(grad.shape, bf16),
        [VMEM] * 4,
        scratch=[
            pltpu.VMEM((ROWS, ROWS), bf16),
            pltpu.VMEM((copies, ROWS, 2 * columns), bf16),
            pltpu.VMEM((rows, 128), f32),
            pltpu.VMEM((ROWS, ROWS), bf16),
        ],
    )(mine, other, gram, own)
    return momentum_out, update


def solution(mesh):
    sizes = (4, 8, 2, 12)
    split_mesh = Mesh(mesh.devices.reshape(sizes), ("x", "y", "core", "group"))
    spec = P("group", ("x", "y", "core"), None)

    def run(grad, momentum):
        entries = grad.size
        layers, flat_rows, _ = grad.shape
        width = flat_rows * 128 // ROWS
        update_scale = 0.2 * math.sqrt(max(ROWS, width))
        return jax.shard_map(
            functools.partial(local, entries, update_scale, sizes),
            mesh=split_mesh,
            in_specs=(spec, spec),
            out_specs=(spec, spec),
            check_vma=False,
        )(grad, momentum)

    return run
```

```python
import functools
import math

import jax
import jax.numpy as jnp
import numpy as np
from jax import lax
from jax.experimental import pallas as pl
from jax.experimental.pallas import tpu as pltpu
from jax.sharding import Mesh, PartitionSpec as P

ROWS = 576
ITERS = 2

momentum_rate = 0.95
target_rms = 0.5
coef_first = 3.4445
coef_second = -4.775
coef_third = 2.0315

f32, bf16 = jnp.float32, jnp.bfloat16
VMEM = pl.BlockSpec(memory_space=pltpu.VMEM)
SMEM = pl.BlockSpec(memory_space=pltpu.SMEM)
NT = (((1,), (1,)), ((), ()))


def two_sum(a, b):
    s = a + b
    t = s - a
    return s, (a - (s - t)) + (b - t)


def fast_two_sum(a, b):
    s = a + b
    return s, b - (s - a)


def split(a):
    t = 4097.0 * a
    high = t - (t - a)
    return high, a - high


def two_prod(a, b):
    p = a * b
    ah, al = split(a)
    bh, bl = split(b)
    return p, ((ah * bh - p) + ah * bl + al * bh) + al * bl


def dd_add(a, b):
    s, e = two_sum(a[0], b[0])
    return fast_two_sum(s, e + (a[1] + b[1]))


def dd_mul(a, b):
    p, e = two_prod(a[0], b[0])
    return fast_two_sum(p, e + (a[0] * b[1] + a[1] * b[0]))


def dd_const(value):
    high = np.float32(value)
    return float(high), float(np.float32(value - float(high)))


def lazy_add(a, b):
    s, e = two_sum(a[0], b[0])
    return s, (a[1] + b[1]) + e


def tree(values):
    while len(values) > 1:
        paired = [lazy_add(values[i], values[i + 1]) for i in range(0, len(values) - 1, 2)]
        values = paired + ([values[-1]] if len(values) % 2 else [])
    return values[0]


def fold(a, axis, shifts):
    for shift in shifts:
        a = lazy_add(a, (pltpu.roll(a[0], shift, axis), pltpu.roll(a[1], shift, axis)))
    return a


def lanes():
    return lax.broadcasted_iota(jnp.int32, (8, 128), 1)


def pack(values):
    lane = lanes()
    tile = jnp.zeros((8, 128), f32)
    for i, (high, low) in enumerate(values):
        tile = jnp.where(lane == i, high, jnp.where(lane == i + 64, low, tile))
    return tile


def add_rows(ref):
    zero = jnp.zeros((8, 128), f32)
    high, low = fold(tree([(ref[i : i + 8, :], zero) for i in range(0, ref.shape[0], 8)]), 0, (4, 2, 1))
    return fast_two_sum(high, low + pltpu.roll(high, 64, 1))


def sums_kernel(groups, group_ref, pair_ref, out_ref):
    gg, gm, mm = [], [], []
    for i in range(0, pair_ref.shape[1], 8):
        g = pair_ref[0, i : i + 8, :]
        m = pair_ref[1, i : i + 8, :]
        gg.append(two_prod(g, g))
        gm.append(two_prod(g, m))
        mm.append(two_prod(m, m))
    sums = [fold(fold(tree(v), 0, (4, 2, 1)), 1, (64, 32, 16, 8, 4, 2, 1)) for v in (gg, gm, mm)]
    tile = pack([fast_two_sum(*v) for v in [sums[0]] + sums])
    for i in range(0, out_ref.shape[0], 8):
        to = lax.rem(lax.broadcasted_iota(jnp.int32, (8, 128), 0) + i, groups)
        keep = (to == group_ref[0]) | (lax.rem(lanes(), 64) == 0)
        out_ref[i : i + 8, :] = jnp.where(keep, tile, 0.0)


def combine_kernel(in_ref, out_ref):
    high, low = add_rows(in_ref)
    tile = jnp.where(lanes() < 64, high, pltpu.roll(low, 64, 1))
    for i in range(0, out_ref.shape[0], 8):
        out_ref[i : i + 8, :] = tile


def scale_kernel(entries, in_ref, pair_ref, out_ref, own_ref, scale_ref):
    high, low = add_rows(in_ref)
    lane = lanes()

    def value(i):
        return tuple(jnp.sum(jnp.where(lane == i, v, 0.0), axis=1, keepdims=True)[0:1] for v in (high, low))

    square, gg, gm, mm = (value(i) for i in range(4))
    grad_scale = target_rms / (jnp.sqrt(square[0] / entries) + 1e-06)
    rate = float(np.float32(momentum_rate))
    factor_high, factor_low = dd_const(1.0 + rate)
    ones = jnp.ones_like(grad_scale)
    a = two_prod(grad_scale, factor_high * ones)
    a = fast_two_sum(a[0], a[1] + grad_scale * factor_low)
    b = tuple(v * ones for v in dd_const(rate * rate))
    cross = dd_mul(dd_mul((2.0 * a[0], 2.0 * a[1]), b), gm)
    total = dd_add(dd_add(dd_mul(a, dd_mul(a, gg)), dd_mul(dd_mul(b, b), mm)), cross)
    unorm = jnp.sqrt(jnp.maximum(total[0], 0.0))
    scaled_grad = grad_scale * pair_ref[0]
    nudged = scaled_grad + momentum_rate * (momentum_rate * pair_ref[1] + scaled_grad)
    iterate = (nudged / (unorm + 1e-07)).astype(bf16)
    for i in range(out_ref.shape[0]):
        out_ref[i] = iterate
    own_ref[...] = iterate.astype(f32)
    scale_ref[...] = jnp.broadcast_to(grad_scale, scale_ref.shape)


def transpose_kernel(copies, in_ref, out_ref, flat_ref):
    blocks, rows = in_ref.shape[:2]
    for i in range(blocks):
        flat_ref[i * rows : (i + 1) * rows, :] = in_ref[i].astype(f32)
    half = blocks * rows // 9
    low = lax.broadcasted_iota(jnp.int32, (half, 128), 1) < 64
    flat = [flat_ref[pl.ds(j, half, stride=9), :] for j in range(9)]
    turned = [pltpu.roll(flat[j], 64, 1) for j in range(4, 9)]
    for j in range(5):
        odd = jnp.where(low, turned[j], turned[j + 1]) if j < 4 else turned[4]
        block = jnp.concatenate([flat[j], odd], 0).T.astype(bf16)
        width = min(128, ROWS - 128 * j)
        for i in range(copies):
            out_ref[i, 128 * j : 128 * j + width, :] = block[:width]


def own_load(flat_ref, pairs):
    low = lax.broadcasted_iota(jnp.int32, (pairs, 128), 1) < 64
    flat = [flat_ref[pl.ds(j, pairs, stride=9), :] for j in range(9)]
    turned = [pltpu.roll(flat[j], 64, 1) for j in range(4, 9)]
    even = flat[:4] + [flat[4]]
    odd = [jnp.where(low, turned[k], turned[k + 1]) for k in range(4)] + [turned[4]]
    return jnp.concatenate([jnp.concatenate(even, 1), jnp.concatenate(odd, 1)], 0)[:, :ROWS]


def own_store(flat_ref, value, pairs):
    value = jnp.concatenate([value, jnp.zeros((2 * pairs, 64), f32)], 1)
    low = lax.broadcasted_iota(jnp.int32, (pairs, 128), 1) < 64
    even = [value[:pairs, 128 * j : 128 * j + 128] for j in range(5)]
    odd = [pltpu.roll(value[pairs:, 128 * j : 128 * j + 128], 64, 1) for j in range(5)]
    flat = even[:4] + [jnp.where(low, even[4], odd[0])]
    flat += [jnp.where(low, odd[k], odd[k + 1]) for k in range(4)]
    for j in range(9):
        flat_ref[pl.ds(j, pairs, stride=9), :] = flat[j]


def triangle():
    return [(a, min(a + 256, ROWS)) for a in range(0, ROWS, 256)]


def side_by_side(values):
    return jnp.concatenate(values, 1)


def gram_columns(iterate):
    return [lax.dot_general(iterate[a:], iterate[a:b], NT, preferred_element_type=f32) for a, b in triangle()]


def mirror(ref, value, a, b):
    ref[a:, a:b] = value
    if b < ROWS:
        ref[a:b, b:] = value[b - a :].T


def store_poly(columns, low_ref, poly_ref):
    for (a, b), column in zip(triangle(), columns):
        mirror(low_ref, column.astype(bf16), a, b)
    for (a, b), column in zip(triangle(), columns):
        squared = jnp.dot(low_ref[a:, :], low_ref[:, a:b], preferred_element_type=f32)
        mirror(poly_ref, (coef_second * column + coef_third * squared).astype(bf16), a, b)


def gram_kernel(mine_ref, pair_ref, scale_ref, gram_ref, momentum_out_ref):
    iterate = side_by_side([mine_ref[i] for i in range(mine_ref.shape[0])])
    for (a, b), column in zip(triangle(), gram_columns(iterate)):
        gram_ref[a:, a:b] = column
    momentum_out_ref[0] = momentum_rate * pair_ref[1] + scale_ref[0:1, :] * pair_ref[0]


def iterate_kernel(update_scale, mine_ref, other_ref, gram_ref, own_ref, out_ref, poly_ref, next_ref, flat_ref, low_ref):
    blocks = [side_by_side([r[i], r[i + 1]]) for r in (mine_ref, other_ref) for i in range(0, r.shape[0], 2)]
    pairs = own_ref.shape[0] // 9
    columns = gram_columns(side_by_side([other_ref[i] for i in range(other_ref.shape[0])]))
    columns = [gram_ref[a:, a:b] + column for (a, b), column in zip(triangle(), columns)]
    store_poly(columns, low_ref, poly_ref)
    for i, v in enumerate(blocks):
        product = jnp.dot(poly_ref[...], v, preferred_element_type=f32)
        next_ref[i] = (coef_first * v.astype(f32) + product).astype(bf16)
    columns = gram_columns(side_by_side([next_ref[i] for i in range(len(blocks))]))
    own = own_load(own_ref, pairs)
    product = jnp.dot(own.astype(bf16), poly_ref[...], preferred_element_type=f32)
    own = (coef_first * own + product).astype(bf16)
    store_poly(columns, low_ref, poly_ref)
    product = side_by_side([jnp.dot(own, poly_ref[:, a:b], preferred_element_type=f32) for a, b in triangle()])
    own_store(flat_ref, update_scale * (coef_first * own.astype(f32) + product), pairs)
    out_ref[0] = flat_ref[...].astype(bf16)


def pairings(count, core):
    return [((i + core) % count, (i + core + 1) % count) for i in range(0, count, 2)]


def gather_groups(nx, ny, nc):
    def at(x, y, core):
        return (x * ny + y) * nc + core

    first, second = [], []
    for core in range(nc):
        for x in range(nx):
            first += [[at(x, y, core) for y in range(parity, ny, 2)] for parity in range(2)]
        second += [[at(x, y, core) for x in range(nx) for y in ys] for ys in pairings(ny, 0)]
    return first, second


def kernel(body, name, out, in_specs, scratch=(), cost=None):
    return pl.pallas_call(
        body,
        name=name,
        out_shape=out,
        in_specs=in_specs,
        out_specs=jax.tree.map(lambda _: VMEM, out),
        scratch_shapes=list(scratch),
        compiler_params=pltpu.CompilerParams(vmem_limit_bytes=40 * 2**20),
        cost_estimate=cost,
    )


def local(entries, update_scale, sizes, grad, momentum):
    nx, ny, nc, ng = sizes
    chips = ("x", "y", "core")
    first_groups, second_groups = gather_groups(nx, ny, nc)
    blocks, copies = len(first_groups[0]), len(second_groups[0])
    rows = grad.shape[1]
    columns = blocks * rows * 128 // ROWS
    shape = jax.ShapeDtypeStruct
    group = lax.axis_index("group").astype(jnp.int32).reshape(1)
    grad, momentum, group = lax.optimization_barrier((grad, momentum, group))
    first = lax.broadcasted_iota(jnp.int32, (2, rows, 128), 0) == 0
    pair = jnp.where(first, grad, momentum)
    sums = kernel(functools.partial(sums_kernel, ng), "sums", shape((nx * ng, 128), f32), [SMEM, VMEM])(group, pair)
    sums = lax.all_to_all(sums.reshape(-1, 1, 128), ("x", "group"), 0, 0).reshape(-1, 128)
    sums = kernel(combine_kernel, "combine", shape((ny * nc, 128), f32), [VMEM])(sums)
    sums = lax.all_to_all(sums.reshape(-1, 1, 128), ("y", "core"), 0, 0).reshape(-1, 128)
    iterate, own, scale = kernel(
        functools.partial(scale_kernel, entries),
        "scale",
        (shape((blocks, rows, 128), bf16), shape((rows, 128), f32), shape((8, 128), f32)),
        [VMEM] * 2,
    )(sums, pair)
    gathered = lax.all_to_all(iterate, chips, 0, 0, axis_index_groups=first_groups)
    turned = kernel(
        functools.partial(transpose_kernel, copies),
        "turn",
        shape((copies, ROWS, columns), bf16),
        [VMEM],
        scratch=[pltpu.VMEM((blocks * rows, 128), f32)],
    )(gathered)
    mine = lax.all_to_all(turned, chips, 0, 0, axis_index_groups=second_groups)
    other = lax.ppermute(mine, "core", [(0, 1), (1, 0)])
    gram, momentum_out = kernel(
        gram_kernel,
        "gram",
        (shape((ROWS, ROWS), f32), shape(grad.shape, f32)),
        [VMEM] * 3,
        cost=pl.CostEstimate(flops=2 * ROWS * ROWS * columns * copies, bytes_accessed=2 * ROWS * columns * copies, transcendentals=0),
    )(mine, pair, scale)
    update = kernel(
        functools.partial(iterate_kernel, update_scale),
        "newton",
        shape(grad.shape, bf16),
        [VMEM] * 4,
        scratch=[
            pltpu.VMEM((ROWS, ROWS), bf16),
            pltpu.VMEM((copies, ROWS, 2 * columns), bf16),
            pltpu.VMEM((rows, 128), f32),
            pltpu.VMEM((ROWS, ROWS), bf16),
        ],
    )(mine, other, gram, own)
    return momentum_out, update


def solution(mesh):
    sizes = (4, 8, 2, 12)
    split_mesh = Mesh(mesh.devices.reshape(sizes), ("x", "y", "core", "group"))
    spec = P("group", ("x", "y", "core"), None)

    def run(grad, momentum):
        entries = grad.size
        layers, flat_rows, _ = grad.shape
        width = flat_rows * 128 // ROWS
        update_scale = 0.2 * math.sqrt(max(ROWS, width))
        return jax.shard_map(
            functools.partial(local, entries, update_scale, sizes),
            mesh=split_mesh,
            in_specs=(spec, spec),
            out_specs=(spec, spec),
            check_vma=False,
        )(grad, momentum)

    return run
```
